256 devices in a mesh: az: 64 (over x, z, core), rg: 4 (over y).
Axes of the slice: x: 4, y: 4, z: 8, core: 2. Of those that a mesh axis runs over, the one named last changes fastest.
Arguments:
- echo_data: float32 [2, 2048, 32768], P(None, 'rg', 'az'), may hold values from -6 to 6
- chirp_phase: float32 [2048], P('rg'), may hold values from -3.140625 to 3.140625
- stolt_shift: int32 [16, 32768], P('rg', 'az'), may hold values from 0 to 64
- tap_index: int32 [16, 32768], P('rg', 'az'), may hold values from 0 to 15
Outputs:
- mapped_spectrum: float32 [2, 2048, 32768], P(None, 'rg', 'az')
The draws below stay inside these ranges and needn't reach their ends.
All inputs are finite; a program needn't handle non-finite values.
Results may differ from the reference program's by a relative error of at most 0.0003.
Values sent between devices are 32-bit elements; how exact they have to be, the bound alone decides.
A program may use at most 64 MiB of HBM per device.

```python
import math
import jax
import jax.numpy as jnp
from jax import lax

AZ_DEV = 512
SHIFT_MAX = 64
FRAC_STEPS = 16
TAP_COUNT = 8
AZ_LEN = 32768
RG_LEN = 2048
SEGMENTS = 16
N_AZ = 64


def draw_stolt_shift(key, part):
    key = jax.random.fold_in(key, 11)
    lines = jnp.arange(AZ_LEN, dtype=jnp.int32)
    folded_line = jnp.minimum(lines, AZ_LEN - lines)
    scaled = folded_line * 1024 // (AZ_LEN // 2)
    base_shift = SHIFT_MAX * scaled * scaled // 1048576
    jitter = jax.random.randint(key, (SEGMENTS, AZ_LEN), 0, SHIFT_MAX // 2 + 1, dtype=jnp.int32)
    return jnp.minimum(base_shift[None, :] + jitter, SHIFT_MAX).astype(jnp.int32)


def with_ends(array, key, low, top_value):
    dims = array.shape
    spot = [jax.random.randint(jax.random.fold_in(key, axis), (), 0, dims[axis]) for axis in range(len(dims))]
    array = array.at[tuple(spot)].set(low)
    longest = dims.index(max(dims))
    spot[longest] = (spot[longest] + 1) % dims[longest]
    return array.at[tuple(spot)].set(top_value)


def block_scale(rng, extent, shards, low, top_value):
    gain = 1.0
    for axis_at, shards_of in shards:
        draws = jax.random.uniform(jax.random.fold_in(jax.random.fold_in(rng, 6), axis_at), (shards_of,), jnp.float32, low / len(shards), top_value / len(shards))
        gain = gain * jnp.repeat(jnp.exp(draws), extent[axis_at] // shards_of).reshape((-1,) + (1,) * (len(extent) - 1 - axis_at))
    return gain


def normal_values(stream_key, extent, width, bound, split=(), held_as=jnp.bfloat16):
    factor_of = block_scale(stream_key, extent, split, -0.22, 0.18) if split else 1.0
    entries = jax.random.normal(stream_key, extent, jnp.float32) * width * factor_of
    return jnp.minimum(jnp.maximum(entries, -bound), bound).astype(held_as)


def setup_inputs(seed: int = 0) -> dict:
    arg_keys = jax.random.split(jax.random.key(seed), 5)
    return {
        "echo_data": normal_values(arg_keys[0], (2, RG_LEN, AZ_LEN), 1.0, 6.0, ((1, 4), (2, 64)), jnp.float32),
        "chirp_phase": jnp.clip(jax.random.uniform(arg_keys[1], (RG_LEN,), jnp.float32, -3.140625, 3.140625), -3.140625, 3.140625),
        "stolt_shift": draw_stolt_shift(jax.random.fold_in(arg_keys[4], 71), 0),
        "tap_index": with_ends(jax.random.randint(arg_keys[3], (SEGMENTS, AZ_LEN), 0, FRAC_STEPS), jax.random.fold_in(arg_keys[3], 1), 0, FRAC_STEPS - 1).astype(jnp.int32),
    }


def stolt_map(extended, shift_table, tap_table, row_count):
    groups, col_count = shift_table.shape
    seg_len = row_count // groups
    row_base = jnp.arange(row_count, dtype=jnp.int32)[:, None]
    shift_rows = jnp.broadcast_to(shift_table[:, None, :], (groups, seg_len, col_count)).reshape(row_count, col_count)
    tap_rows = jnp.broadcast_to(tap_table[:, None, :], (groups, seg_len, col_count)).reshape(row_count, col_count)
    frac_rows = tap_rows.astype(jnp.float32) * (1.0 / FRAC_STEPS)
    accumulated = jnp.zeros((2, row_count, col_count), jnp.float32)
    for tap_slot in range(TAP_COUNT):
        position = row_base + shift_rows + tap_slot
        gather_index = jnp.broadcast_to(position[None], (2, row_count, col_count))
        picked = jnp.take_along_axis(extended, gather_index, axis=1)
        offset = tap_slot - 3.0 - frac_rows
        weight = jnp.sinc(offset) * (0.54 + 0.46 * jnp.cos(offset * (math.pi / 4.0)))
        accumulated = accumulated + weight[None] * picked
    return accumulated

def reference(echo_data, chirp_phase, stolt_shift, tap_index):
    cosine = jnp.cos(chirp_phase)[:, None]
    sine = jnp.sin(chirp_phase)[:, None]
    real_part = echo_data[0] * cosine + echo_data[1] * sine
    imag_part = echo_data[1] * cosine - echo_data[0] * sine
    signal = real_part + 1j * imag_part
    spectrum = jnp.fft.fft(signal, axis=1) * (1.0 / math.sqrt(AZ_LEN))
    spec_real = jnp.real(spectrum)
    spec_imag = jnp.imag(spectrum)
    half_len = AZ_LEN // 2
    range_rows = jnp.arange(RG_LEN, dtype=jnp.int32)
    range_freq = 1.0 + range_rows.astype(jnp.float32) * (1.0 / RG_LEN)

    def one_block(block_id):
        start = block_id * AZ_DEV
        block_real = lax.dynamic_slice_in_dim(spec_real, start, AZ_DEV, 1)
        block_imag = lax.dynamic_slice_in_dim(spec_imag, start, AZ_DEV, 1)
        lines = start + jnp.arange(AZ_DEV, dtype=jnp.int32)
        signed = jnp.where(lines < half_len, lines, lines - AZ_LEN)
        azim_freq = signed.astype(jnp.float32) * (0.9 / half_len)
        phase_angle = 40.0 * jnp.sqrt(range_freq[:, None] * range_freq[:, None] - azim_freq[None, :] * azim_freq[None, :])
        cos_phase = jnp.cos(phase_angle)
        sin_phase = jnp.sin(phase_angle)
        focus_real = block_real * cos_phase - block_imag * sin_phase
        focus_imag = block_real * sin_phase + block_imag * cos_phase
        extended = jnp.pad(jnp.stack([focus_real, focus_imag]), ((0, 0), (3, SHIFT_MAX + 4), (0, 0)))
        shift_block = lax.dynamic_slice_in_dim(stolt_shift, start, AZ_DEV, 1)
        tap_block = lax.dynamic_slice_in_dim(tap_index, start, AZ_DEV, 1)
        return stolt_map(extended, shift_block, tap_block, RG_LEN)
    blocks = lax.map(one_block, jnp.arange(N_AZ, dtype=jnp.int32))
    return jnp.transpose(blocks, (1, 2, 0, 3)).reshape(2, RG_LEN, AZ_LEN)
```

```python
import math

import jax
import jax.numpy as jnp
import numpy as np
from jax import lax
from jax.experimental import pallas as pl
from jax.experimental.pallas import tpu as pltpu
from jax.sharding import PartitionSpec as P

MESH = pl.DeviceIdType.MESH
N_AZ = 64
N_RG = 4
ROWS = 512
COLS = 512
FULL = N_AZ * COLS
LANES = 128
FIRST = 256
SECOND = 128
CHUNKS = 4
CHUNK_ROWS = ROWS // CHUNKS
PAIR = CHUNK_ROWS // N_AZ
BLOCK = PAIR * 8
CHUNK_FLAT = N_AZ * BLOCK
FLAT = CHUNKS * CHUNK_FLAT
BEFORE = 8
AFTER = 72
FOCUS_ROWS = BEFORE + ROWS + AFTER + 8
TAPS = 15
EARLY = 7


def split(array):
    high = array.astype(jnp.bfloat16)
    low = (array - np.asarray(high).astype(np.float64)).astype(jnp.bfloat16)
    return high, low


def dft_tables():
    a = np.arange(FIRST)
    angle = 2.0 * np.pi * (np.outer(a, a) % FIRST) / FIRST
    cosine = np.cos(angle).reshape(FIRST, N_AZ, 4)
    sine = np.sin(angle).reshape(FIRST, N_AZ, 4)
    first = np.stack(
        [np.stack([cosine, sine], axis=2), np.stack([-sine, cosine], axis=2)], axis=0
    ).reshape(2 * FIRST, N_AZ * 8)
    angle = 2.0 * np.pi * (np.outer(a, np.arange(SECOND)) % FULL) / FULL
    norm = 1.0 / math.sqrt(FULL)
    twiddle = np.stack([np.cos(angle), np.sin(angle)]) * norm
    b = np.arange(SECOND)
    angle = 2.0 * np.pi * (np.outer(b, b) % SECOND) / SECOND
    cosine = np.cos(angle).reshape(N_AZ, 2, SECOND).transpose(1, 0, 2)
    sine = np.sin(angle).reshape(N_AZ, 2, SECOND).transpose(1, 0, 2)
    second = np.stack(
        [np.concatenate([cosine, sine], axis=2), np.concatenate([-sine, cosine], axis=2)], axis=0
    ).reshape(2 * SECOND, 2 * SECOND)
    first_high, first_low = split(first)
    second_high, second_low = split(second)
    return first_high, first_low, second_high, second_low, twiddle.astype(np.float32)


def sin_cos_of(rest, count):
    sign = 1.0 - 2.0 * (count - 2.0 * jnp.floor(count * 0.5))
    square = rest * rest
    sine = -1.0 / math.factorial(11)
    for order in (9, 7, 5, 3, 1):
        sine = sine * square + (-1.0) ** (order // 2) / math.factorial(order)
    cosine = 1.0 / math.factorial(12)
    for order in (10, 8, 6, 4, 2, 0):
        cosine = cosine * square + (-1.0) ** (order // 2) / math.factorial(order)
    return sine * rest * sign, cosine * sign


def sin_cos(angle):
    count = jnp.floor(angle * (1.0 / math.pi) + 0.5)
    rest = (angle - count * 3.140625) - count * (math.pi - 3.140625)
    return sin_cos_of(rest, count)


def sin_cos_pi(turns):
    count = jnp.floor(turns + 0.5)
    return sin_cos_of((turns - count) * math.pi, count)


def dot3(table_high, table_low, value, contract_on):
    high = value.astype(jnp.bfloat16)
    low = (value - high.astype(jnp.float32)).astype(jnp.bfloat16)
    dims = (((1,), (contract_on,)), ((), ()))
    dot = lambda left, right: lax.dot_general(left, right, dims, preferred_element_type=jnp.float32)
    return dot(table_high, high) + (dot(table_high, low) + dot(table_low, high))


def kernel(
    echo_hbm, chirp_ref, shift_ref, tap_ref, t1h_hbm, t1l_hbm, t2h_hbm, t2l_hbm, tw_hbm,
    out_ref,
    echo, t1h, t1l, t2h, t2l, tw, out_flat, in_flat, spec_flat, back_flat, phase_cos, phase_sin,
    focus, weights, coarse, chirp_cos, chirp_sin, window,
    load_sem, table_sem, send1, recv1, send2, recv2, halo_send, halo_recv,
):
    me = lax.axis_index("az")
    rg = lax.axis_index("rg")
    up = lax.rem(rg + 1, N_RG)
    down = lax.rem(rg + N_RG - 1, N_RG)

    barrier = pltpu.get_barrier_semaphore()

    def greet(i, carry):
        pl.semaphore_signal(
            barrier, inc=1, device_id=(lax.rem(me + i, N_AZ), rg), device_id_type=MESH
        )
        return carry

    echo_copies = []
    for chunk in range(CHUNKS):
        rows = pl.ds(chunk * CHUNK_ROWS, CHUNK_ROWS)
        echo_copies.append(
            pltpu.make_async_copy(echo_hbm.at[:, rows], echo.at[:, rows], load_sem.at[chunk])
        )
        echo_copies[-1].start()
    lax.fori_loop(1, N_AZ, greet, 0)
    for other in (up, down):
        pl.semaphore_signal(barrier, inc=1, device_id=(me, other), device_id_type=MESH)
    table_copies = []
    for index, (source, target) in enumerate(
        ((t1h_hbm, t1h), (t1l_hbm, t1l), (t2h_hbm, t2h), (t2l_hbm, t2l), (tw_hbm, tw))
    ):
        table_copies.append(pltpu.make_async_copy(source, target, table_sem.at[index]))
        table_copies[-1].start()

    sine, cosine = sin_cos_pi(chirp_ref[...] * (1.0 / math.pi))
    for part in range(ROWS // LANES):
        rows = pl.ds(part * LANES, LANES)
        chirp_cos[rows, :] = jnp.transpose(
            jnp.broadcast_to(cosine[part : part + 1, :], (LANES, LANES))
        )
        chirp_sin[rows, :] = jnp.transpose(
            jnp.broadcast_to(sine[part : part + 1, :], (LANES, LANES))
        )

    def matched(chunk):
        def body(i, carry):
            row = pl.multiple_of(chunk * CHUNK_ROWS + i * 8, 8)
            c = chirp_cos[pl.ds(row, 8), :]
            s = chirp_sin[pl.ds(row, 8), :]
            for tile in range(4):
                lanes = slice(tile * LANES, (tile + 1) * LANES)
                re = echo[0, pl.ds(row, 8), lanes]
                im = echo[1, pl.ds(row, 8), lanes]
                out_flat[pl.ds(row * 8 + tile, 8, stride=8), :] = re * c + im * s
                out_flat[pl.ds(row * 8 + 4 + tile, 8, stride=8), :] = im * c - re * s
            return carry

        lax.fori_loop(0, CHUNK_ROWS // 8, body, 0)

    def exchange(source, target, send, recv, chunk):
        def body(i, carry):
            other = lax.rem(me + i, N_AZ)
            away = pl.multiple_of(chunk * CHUNK_FLAT + other * BLOCK, BLOCK)
            home = pl.multiple_of(chunk * CHUNK_FLAT + me * BLOCK, BLOCK)
            pltpu.make_async_remote_copy(
                src_ref=source.at[pl.ds(away, BLOCK)],
                dst_ref=target.at[pl.ds(home, BLOCK)],
                send_sem=send.at[chunk],
                recv_sem=recv.at[chunk],
                device_id=(other, rg),
                device_id_type=MESH,
            ).start()
            return carry

        lax.fori_loop(1, N_AZ, body, 0)
        home = pl.multiple_of(chunk * CHUNK_FLAT + me * BLOCK, BLOCK)
        target[pl.ds(home, BLOCK), :] = source[pl.ds(home, BLOCK), :]

    def all_of(source, target, send, recv, chunk):
        rows = pl.ds(pl.multiple_of(chunk * CHUNK_FLAT, BLOCK), CHUNK_FLAT - BLOCK)
        return pltpu.make_async_remote_copy(
            src_ref=source.at[rows],
            dst_ref=target.at[rows],
            send_sem=send.at[chunk],
            recv_sem=recv.at[chunk],
            device_id=(lax.rem(me + 1, N_AZ), rg),
            device_id_type=MESH,
        )

    for chunk in range(CHUNKS):
        echo_copies[chunk].wait()
        matched(chunk)
        if chunk == 0:
            pl.semaphore_wait(barrier, N_AZ + 1)
        exchange(out_flat, in_flat, send1, recv1, chunk)

    lane_id = lax.broadcasted_iota(jnp.int32, (8, LANES), 1)
    row_id = lax.broadcasted_iota(jnp.int32, (8, LANES), 0)

    def phase_body(i, carry):
        row = pl.multiple_of(i * 8, 8)
        r = 1.0 + (rg * ROWS + row + row_id).astype(jnp.float32) * (1.0 / (ROWS * N_RG))
        rr = r * r
        for tile in range(4):
            line = me * COLS + tile * LANES + lane_id
            signed = jnp.where(line < FULL // 2, line, line - FULL)
            q = signed.astype(jnp.float32) * (0.9 / (FULL // 2))
            s, c = sin_cos(40.0 * jnp.sqrt(rr - q * q))
            phase_cos[tile, pl.ds(row, 8), :] = c
            phase_sin[tile, pl.ds(row, 8), :] = s
        return carry

    lax.fori_loop(0, ROWS // 8, phase_body, 0)

    tap_id = lax.broadcasted_iota(jnp.int32, (16, LANES), 0)
    for seg in range(CHUNKS):
        for tile in range(4):
            lanes = slice(tile * LANES, (tile + 1) * LANES)
            shift = shift_ref[seg : seg + 1, lanes]
            slot = tap_id - jnp.broadcast_to(shift & 7, (16, LANES))
            frac = jnp.broadcast_to(tap_ref[seg : seg + 1, lanes], (16, LANES))
            u = (slot - 3).astype(jnp.float32) - frac.astype(jnp.float32) * (1.0 / 16.0)
            sine, _ = sin_cos_pi(u)
            _, cosine = sin_cos_pi(u * 0.25)
            at_zero = u == 0.0
            sinc = jnp.where(at_zero, 1.0, sine / jnp.where(at_zero, 1.0, u * math.pi))
            inside = jnp.logical_and(slot >= 0, slot < 8)
            weights[seg * 4 + tile] = jnp.where(inside, sinc * (0.54 + 0.46 * cosine), 0.0)
            coarse[seg * 4 + tile] = jnp.broadcast_to(shift >> 3, (8, LANES))

    for plane in range(8):
        focus[plane, pl.ds(BEFORE, ROWS), :] = jnp.zeros((ROWS, LANES), jnp.float32)
        focus[plane, pl.ds(BEFORE + ROWS + AFTER, 8), :] = jnp.zeros((8, LANES), jnp.float32)

    for copy in table_copies:
        copy.wait()

    def transform(chunk, carry):
        all_of(out_flat, in_flat, send1, recv1, chunk).wait_recv()
        start = pl.multiple_of(chunk * CHUNK_FLAT, CHUNK_FLAT)
        both = in_flat[pl.ds(start, CHUNK_FLAT), :].reshape(N_AZ, PAIR, 8, LANES)
        signal = jnp.concatenate(
            [both[:, pair].reshape(N_AZ * 8, LANES) for pair in range(PAIR)], axis=1
        )
        section = dot3(t1h[...], t1l[...], signal, 0)
        for pair in range(PAIR):
            lanes = slice(pair * LANES, (pair + 1) * LANES)
            re = section[:FIRST, lanes]
            im = section[FIRST:, lanes]
            turned = jnp.concatenate([re * tw[0] + im * tw[1], im * tw[0] - re * tw[1]], axis=1)
            final = dot3(t2h[...], t2l[...], turned, 1)
            for quarter in range(4):
                for half in range(2):
                    spec_flat[pl.ds(start + pair * 8 + quarter * 2 + half, N_AZ, stride=BLOCK), :] = (
                        final[quarter * N_AZ : (quarter + 1) * N_AZ, half * LANES : (half + 1) * LANES]
                    )
        exchange(spec_flat, back_flat, send2, recv2, chunk)
        return carry

    lax.fori_loop(0, CHUNKS, transform, 0)

    def focus_rows(chunk):
        all_of(spec_flat, back_flat, send2, recv2, chunk).wait_recv()

        def body(i, carry):
            row = pl.multiple_of(chunk * CHUNK_ROWS + i * 8, 8)
            for tile in range(4):
                a = back_flat[pl.ds(row * 8 + tile, 8, stride=8), :]
                b = back_flat[pl.ds(row * 8 + 4 + tile, 8, stride=8), :]
                c = phase_cos[tile, pl.ds(row, 8), :]
                s = phase_sin[tile, pl.ds(row, 8), :]
                focus[tile, pl.ds(BEFORE + row, 8), :] = a * c - b * s
                focus[4 + tile, pl.ds(BEFORE + row, 8), :] = a * s + b * c
            return carry

        lax.fori_loop(0, CHUNK_ROWS // 8, body, 0)

    def stolt(seg, first, count):
        def body(tile, carry):
            index = seg * 4 + tile
            h = coarse[index]
            eight = h >= 8
            four = (h & 4) != 0
            two = (h & 2) != 0
            one = (h & 1) != 0
            taps = [jnp.broadcast_to(weights[index, m : m + 1, :], (8, LANES)) for m in range(TAPS)]
            for part in range(2):
                plane = part * 4 + tile
                need = count + 3
                base = pl.multiple_of((seg * 16 + first) * 8, 8)
                load = lambda i: focus[plane, pl.ds(base + i * 8, 8), :]
                tiles = [load(i) for i in range(need + 8)]
                step = [
                    jnp.where(eight, tiles[i + 8], tiles[i]) if i < need else tiles[i]
                    for i in range(need + 7)
                ]
                step = [jnp.where(four, step[i + 4], step[i]) for i in range(need + 3)]
                step = [jnp.where(two, step[i + 2], step[i]) for i in range(need + 1)]
                for i in range(need):
                    window[part, i * 8 : i * 8 + 8, :] = jnp.where(one, step[i + 1], step[i])
                for i in range(count):
                    total = None
                    for m in range(TAPS):
                        term = taps[m] * window[part, i * 8 + 5 + m : i * 8 + 13 + m, :]
                        total = term if total is None else total + term
                    out_ref[part, pl.ds(base + i * 8, 8), pl.ds(pl.multiple_of(tile * LANES, LANES), LANES)] = total
            return carry

        lax.fori_loop(0, 4, body, 0)

    def halo(towards, source_row, target_row, count, which):
        return pltpu.make_async_remote_copy(
            src_ref=focus.at[:, pl.ds(source_row, count)],
            dst_ref=focus.at[:, pl.ds(target_row, count)],
            send_sem=halo_send.at[which],
            recv_sem=halo_recv.at[which],
            device_id=(me, towards),
            device_id_type=MESH,
        )

    to_down = halo(down, BEFORE, BEFORE + ROWS, AFTER, 0)
    to_up = halo(up, BEFORE + ROWS - 8, 0, 8, 1)

    focus_rows(0)
    to_down.start()
    stolt(0, 1, EARLY - 1)

    def middle(chunk, carry):
        focus_rows(chunk)
        stolt(chunk - 1, EARLY, 16 - EARLY)
        stolt(chunk, 0, EARLY)
        return carry

    lax.fori_loop(1, CHUNKS - 1, middle, 0)
    focus_rows(CHUNKS - 1)
    to_up.start()
    stolt(CHUNKS - 2, EARLY, 16 - EARLY)
    to_down.wait_recv()

    @pl.when(rg == N_RG - 1)
    def _():
        focus[:, pl.ds(BEFORE + ROWS, AFTER), :] = jnp.zeros((8, AFTER, LANES), jnp.float32)

    stolt(CHUNKS - 1, 0, EARLY)
    stolt(CHUNKS - 1, EARLY, 16 - EARLY)
    to_up.wait_recv()

    @pl.when(rg == 0)
    def _():
        focus[:, pl.ds(0, BEFORE), :] = jnp.zeros((8, BEFORE, LANES), jnp.float32)

    stolt(0, 0, 1)
    to_down.wait_send()
    to_up.wait_send()
    for chunk in range(CHUNKS):
        all_of(out_flat, in_flat, send1, recv1, chunk).wait_send()
        all_of(spec_flat, back_flat, send2, recv2, chunk).wait_send()


def on_device(echo_data, chirp_phase, stolt_shift, tap_index):
    tables = [jnp.asarray(table) for table in dft_tables()]
    any_spec = pl.BlockSpec(memory_space=pl.ANY)
    vmem_spec = pl.BlockSpec(memory_space=pltpu.VMEM)
    f32 = jnp.float32
    return pl.pallas_call(
        kernel,
        out_shape=jax.ShapeDtypeStruct((2, ROWS, COLS), f32),
        in_specs=[any_spec, vmem_spec, vmem_spec, vmem_spec] + [any_spec] * 5,
        out_specs=vmem_spec,
        scratch_shapes=[
            pltpu.VMEM((2, ROWS, COLS), f32),
            pltpu.VMEM((512, 512), jnp.bfloat16),
            pltpu.VMEM((512, 512), jnp.bfloat16),
            pltpu.VMEM((256, 256), jnp.bfloat16),
            pltpu.VMEM((256, 256), jnp.bfloat16),
            pltpu.VMEM((2, FIRST, SECOND), f32),
            pltpu.VMEM((FLAT, LANES), f32),
            pltpu.VMEM((FLAT, LANES), f32),
            pltpu.VMEM((FLAT, LANES), f32),
            pltpu.VMEM((FLAT, LANES), f32),
            pltpu.VMEM((4, ROWS, LANES), f32),
            pltpu.VMEM((4, ROWS, LANES), f32),
            pltpu.VMEM((8, FOCUS_ROWS, LANES), f32),
            pltpu.VMEM((16, 16, LANES), f32),
            pltpu.VMEM((16, 8, LANES), jnp.int32),
            pltpu.VMEM((ROWS, LANES), f32),
            pltpu.VMEM((ROWS, LANES), f32),
            pltpu.VMEM((2, 160, LANES), f32),
            pltpu.SemaphoreType.DMA((CHUNKS,)),
            pltpu.SemaphoreType.DMA((5,)),
            pltpu.SemaphoreType.DMA((CHUNKS,)),
            pltpu.SemaphoreType.DMA((CHUNKS,)),
            pltpu.SemaphoreType.DMA((CHUNKS,)),
            pltpu.SemaphoreType.DMA((CHUNKS,)),
            pltpu.SemaphoreType.DMA((2,)),
            pltpu.SemaphoreType.DMA((2,)),
        ],
        compiler_params=pltpu.CompilerParams(
            collective_id=0, has_side_effects=True, vmem_limit_bytes=48 << 20
        ),
    )(echo_data, chirp_phase.reshape(ROWS // LANES, LANES), stolt_shift, tap_index, *tables)


def solution(mesh):
    return jax.shard_map(
        on_device,
        mesh=mesh,
        in_specs=(P(None, "rg", "az"), P("rg"), P("rg", "az"), P("rg", "az")),
        out_specs=P(None, "rg", "az"),
        check_vma=False,
    )
```

```python
import math

import jax
import jax.numpy as jnp
import numpy as np
from jax import lax
from jax.experimental import pallas as pl
from jax.experimental.pallas import tpu as pltpu
from jax.sharding import PartitionSpec as P

MESH = pl.DeviceIdType.MESH
N_AZ = 64
N_RG = 4
ROWS = 512
COLS = 512
FULL = N_AZ * COLS
LANES = 128
FIRST = 256
SECOND = 128
CHUNKS = 4
CHUNK_ROWS = ROWS // CHUNKS
PAIR = CHUNK_ROWS // N_AZ
BLOCK = PAIR * 8
CHUNK_FLAT = N_AZ * BLOCK
FLAT = CHUNKS * CHUNK_FLAT
BEFORE = 8
AFTER = 72
FOCUS_ROWS = BEFORE + ROWS + AFTER + 8
TAPS = 15
EARLY = 7


def split(array):
    high = array.astype(jnp.bfloat16)
    low = (array - np.asarray(high).astype(np.float64)).astype(jnp.bfloat16)
    return high, low


def dft_tables():
    a = np.arange(FIRST)
    angle = 2.0 * np.pi * (np.outer(a, a) % FIRST) / FIRST
    cosine = np.cos(angle).reshape(FIRST, N_AZ, 4)
    sine = np.sin(angle).reshape(FIRST, N_AZ, 4)
    first = np.stack(
        [np.stack([cosine, sine], axis=2), np.stack([-sine, cosine], axis=2)], axis=0
    ).reshape(2 * FIRST, N_AZ * 8)
    angle = 2.0 * np.pi * (np.outer(a, np.arange(SECOND)) % FULL) / FULL
    norm = 1.0 / math.sqrt(FULL)
    twiddle = np.stack([np.cos(angle), np.sin(angle)]) * norm
    b = np.arange(SECOND)
    angle = 2.0 * np.pi * (np.outer(b, b) % SECOND) / SECOND
    cosine = np.cos(angle).reshape(N_AZ, 2, SECOND).transpose(1, 0, 2)
    sine = np.sin(angle).reshape(N_AZ, 2, SECOND).transpose(1, 0, 2)
    second = np.stack(
        [np.concatenate([cosine, sine], axis=2), np.concatenate([-sine, cosine], axis=2)], axis=0
    ).reshape(2 * SECOND, 2 * SECOND)
    first_high, first_low = split(first)
    second_high, second_low = split(second)
    return first_high, first_low, second_high, second_low, twiddle.astype(np.float32)


def sin_cos_of(rest, count):
    sign = 1.0 - 2.0 * (count - 2.0 * jnp.floor(count * 0.5))
    square = rest * rest
    sine = -1.0 / math.factorial(11)
    for order in (9, 7, 5, 3, 1):
        sine = sine * square + (-1.0) ** (order // 2) / math.factorial(order)
    cosine = 1.0 / math.factorial(12)
    for order in (10, 8, 6, 4, 2, 0):
        cosine = cosine * square + (-1.0) ** (order // 2) / math.factorial(order)
    return sine * rest * sign, cosine * sign


def sin_cos(angle):
    count = jnp.floor(angle * (1.0 / math.pi) + 0.5)
    rest = (angle - count * 3.140625) - count * (math.pi - 3.140625)
    return sin_cos_of(rest, count)


def sin_cos_pi(turns):
    count = jnp.floor(turns + 0.5)
    return sin_cos_of((turns - count) * math.pi, count)


def dot3(table_high, table_low, value, contract_on):
    high = value.astype(jnp.bfloat16)
    low = (value - high.astype(jnp.float32)).astype(jnp.bfloat16)
    dims = (((1,), (contract_on,)), ((), ()))
    dot = lambda left, right: lax.dot_general(left, right, dims, preferred_element_type=jnp.float32)
    return dot(table_high, high) + (dot(table_high, low) + dot(table_low, high))


def kernel(
    echo_hbm, chirp_hbm, shift_hbm, tap_hbm, t1h_hbm, t1l_hbm, t2h_hbm, t2l_hbm, tw_hbm,
    out_hbm,
    out_ref, echo, chirp_ref, shift_ref, tap_ref, t1h, t1l, t2h, t2l, tw, out_flat, in_flat, spec_flat, back_flat, phase_cos, phase_sin,
    focus, weights, coarse, chirp_cos, chirp_sin, window,
    load_sem, table_sem, store_sem, send1, recv1, send2, recv2, halo_send, halo_recv,
):
    me = lax.axis_index("az")
    rg = lax.axis_index("rg")
    up = lax.rem(rg + 1, N_RG)
    down = lax.rem(rg + N_RG - 1, N_RG)

    barrier = pltpu.get_barrier_semaphore()

    def greet(i, carry):
        pl.semaphore_signal(
            barrier, inc=1, device_id=(lax.rem(me + i, N_AZ), rg), device_id_type=MESH
        )
        return carry

    chirp_copy = pltpu.make_async_copy(chirp_hbm, chirp_ref, table_sem.at[5])
    chirp_copy.start()
    echo_copies = []
    for chunk in range(CHUNKS):
        rows = pl.ds(chunk * CHUNK_ROWS, CHUNK_ROWS)
        echo_copies.append(
            pltpu.make_async_copy(echo_hbm.at[:, rows], echo.at[:, rows], load_sem.at[chunk])
        )
        echo_copies[-1].start()
    lax.fori_loop(1, N_AZ, greet, 0)
    for other in (up, down):
        pl.semaphore_signal(barrier, inc=1, device_id=(me, other), device_id_type=MESH)
    table_copies = []
    for index, (source, target) in enumerate(
        (
            (t1h_hbm, t1h), (t1l_hbm, t1l), (t2h_hbm, t2h), (t2l_hbm, t2l), (tw_hbm, tw),
        )
    ):
        table_copies.append(pltpu.make_async_copy(source, target, table_sem.at[index]))
        table_copies[-1].start()

    shift_copy = pltpu.make_async_copy(shift_hbm, shift_ref, table_sem.at[6])
    tap_copy = pltpu.make_async_copy(tap_hbm, tap_ref, table_sem.at[7])
    shift_copy.start()
    tap_copy.start()

    chirp_copy.wait()
    sine, cosine = sin_cos_pi(chirp_ref[...] * (1.0 / math.pi))
    for part in range(ROWS // LANES):
        rows = pl.ds(part * LANES, LANES)
        chirp_cos[rows, :] = jnp.transpose(
            jnp.broadcast_to(cosine[part : part + 1, :], (LANES, LANES))
        )
        chirp_sin[rows, :] = jnp.transpose(
            jnp.broadcast_to(sine[part : part + 1, :], (LANES, LANES))
        )

    def matched(chunk):
        def body(i, carry):
            row = pl.multiple_of(chunk * CHUNK_ROWS + i * 8, 8)
            c = chirp_cos[pl.ds(row, 8), :]
            s = chirp_sin[pl.ds(row, 8), :]
            for tile in range(4):
                lanes = slice(tile * LANES, (tile + 1) * LANES)
                re = echo[0, pl.ds(row, 8), lanes]
                im = echo[1, pl.ds(row, 8), lanes]
                out_flat[pl.ds(row * 8 + tile, 8, stride=8), :] = re * c + im * s
                out_flat[pl.ds(row * 8 + 4 + tile, 8, stride=8), :] = im * c - re * s
            return carry

        lax.fori_loop(0, CHUNK_ROWS // 8, body, 0)

    def exchange(source, target, send, recv, chunk):
        def body(i, carry):
            other = lax.rem(me + i, N_AZ)
            away = pl.multiple_of(chunk * CHUNK_FLAT + other * BLOCK, BLOCK)
            home = pl.multiple_of(chunk * CHUNK_FLAT + me * BLOCK, BLOCK)
            pltpu.make_async_remote_copy(
                src_ref=source.at[pl.ds(away, BLOCK)],
                dst_ref=target.at[pl.ds(home, BLOCK)],
                send_sem=send.at[chunk],
                recv_sem=recv.at[chunk],
                device_id=(other, rg),
                device_id_type=MESH,
            ).start()
            return carry

        lax.fori_loop(1, N_AZ, body, 0)
        home = pl.multiple_of(chunk * CHUNK_FLAT + me * BLOCK, BLOCK)
        target[pl.ds(home, BLOCK), :] = source[pl.ds(home, BLOCK), :]

    def all_of(source, target, send, recv, chunk):
        rows = pl.ds(pl.multiple_of(chunk * CHUNK_FLAT, BLOCK), CHUNK_FLAT - BLOCK)
        return pltpu.make_async_remote_copy(
            src_ref=source.at[rows],
            dst_ref=target.at[rows],
            send_sem=send.at[chunk],
            recv_sem=recv.at[chunk],
            device_id=(lax.rem(me + 1, N_AZ), rg),
            device_id_type=MESH,
        )

    for chunk in range(CHUNKS):
        echo_copies[chunk].wait()
        matched(chunk)
        if chunk == 0:
            pl.semaphore_wait(barrier, N_AZ + 1)
        exchange(out_flat, in_flat, send1, recv1, chunk)

    lane_id = lax.broadcasted_iota(jnp.int32, (8, LANES), 1)
    row_id = lax.broadcasted_iota(jnp.int32, (8, LANES), 0)

    def phase_body(i, carry):
        row = pl.multiple_of(i * 8, 8)
        r = 1.0 + (rg * ROWS + row + row_id).astype(jnp.float32) * (1.0 / (ROWS * N_RG))
        rr = r * r
        for tile in range(4):
            line = me * COLS + tile * LANES + lane_id
            signed = jnp.where(line < FULL // 2, line, line - FULL)
            q = signed.astype(jnp.float32) * (0.9 / (FULL // 2))
            s, c = sin_cos(40.0 * jnp.sqrt(rr - q * q))
            phase_cos[tile, pl.ds(row, 8), :] = c
            phase_sin[tile, pl.ds(row, 8), :] = s
        return carry

    lax.fori_loop(0, ROWS // 8, phase_body, 0)

    shift_copy.wait()
    tap_copy.wait()
    tap_id = lax.broadcasted_iota(jnp.int32, (16, LANES), 0)
    for seg in range(CHUNKS):
        for tile in range(4):
            lanes = slice(tile * LANES, (tile + 1) * LANES)
            shift = shift_ref[seg : seg + 1, lanes]
            slot = tap_id - jnp.broadcast_to(shift & 7, (16, LANES))
            frac = jnp.broadcast_to(tap_ref[seg : seg + 1, lanes], (16, LANES))
            u = (slot - 3).astype(jnp.float32) - frac.astype(jnp.float32) * (1.0 / 16.0)
            sine, _ = sin_cos_pi(u)
            _, cosine = sin_cos_pi(u * 0.25)
            at_zero = u == 0.0
            sinc = jnp.where(at_zero, 1.0, sine / jnp.where(at_zero, 1.0, u * math.pi))
            inside = jnp.logical_and(slot >= 0, slot < 8)
            weights[seg * 4 + tile] = jnp.where(inside, sinc * (0.54 + 0.46 * cosine), 0.0)
            coarse[seg * 4 + tile] = jnp.broadcast_to(shift >> 3, (8, LANES))

    for plane in range(8):
        focus[plane, pl.ds(BEFORE, ROWS), :] = jnp.zeros((ROWS, LANES), jnp.float32)
        focus[plane, pl.ds(BEFORE + ROWS + AFTER, 8), :] = jnp.zeros((8, LANES), jnp.float32)

    for copy in table_copies:
        copy.wait()

    def transform(chunk, carry):
        all_of(out_flat, in_flat, send1, recv1, chunk).wait_recv()
        start = pl.multiple_of(chunk * CHUNK_FLAT, CHUNK_FLAT)
        both = in_flat[pl.ds(start, CHUNK_FLAT), :].reshape(N_AZ, PAIR, 8, LANES)
        signal = jnp.concatenate(
            [both[:, pair].reshape(N_AZ * 8, LANES) for pair in range(PAIR)], axis=1
        )
        section = dot3(t1h[...], t1l[...], signal, 0)
        for pair in range(PAIR):
            lanes = slice(pair * LANES, (pair + 1) * LANES)
            re = section[:FIRST, lanes]
            im = section[FIRST:, lanes]
            turned = jnp.concatenate([re * tw[0] + im * tw[1], im * tw[0] - re * tw[1]], axis=1)
            final = dot3(t2h[...], t2l[...], turned, 1)
            for quarter in range(4):
                for half in range(2):
                    spec_flat[pl.ds(start + pair * 8 + quarter * 2 + half, N_AZ, stride=BLOCK), :] = (
                        final[quarter * N_AZ : (quarter + 1) * N_AZ, half * LANES : (half + 1) * LANES]
                    )
        exchange(spec_flat, back_flat, send2, recv2, chunk)
        return carry

    lax.fori_loop(0, CHUNKS, transform, 0)

    def focus_rows(chunk):
        all_of(spec_flat, back_flat, send2, recv2, chunk).wait_recv()

        def body(i, carry):
            row = pl.multiple_of(chunk * CHUNK_ROWS + i * 8, 8)
            for tile in range(4):
                a = back_flat[pl.ds(row * 8 + tile, 8, stride=8), :]
                b = back_flat[pl.ds(row * 8 + 4 + tile, 8, stride=8), :]
                c = phase_cos[tile, pl.ds(row, 8), :]
                s = phase_sin[tile, pl.ds(row, 8), :]
                focus[tile, pl.ds(BEFORE + row, 8), :] = a * c - b * s
                focus[4 + tile, pl.ds(BEFORE + row, 8), :] = a * s + b * c
            return carry

        lax.fori_loop(0, CHUNK_ROWS // 8, body, 0)

    def stolt(seg, first, count):
        def body(tile, carry):
            index = seg * 4 + tile
            h = coarse[index]
            eight = h >= 8
            four = (h & 4) != 0
            two = (h & 2) != 0
            one = (h & 1) != 0
            taps = [jnp.broadcast_to(weights[index, m : m + 1, :], (8, LANES)) for m in range(TAPS)]
            for part in range(2):
                plane = part * 4 + tile
                need = count + 3
                base = pl.multiple_of((seg * 16 + first) * 8, 8)
                load = lambda i: focus[plane, pl.ds(base + i * 8, 8), :]
                tiles = [load(i) for i in range(need + 8)]
                step = [
                    jnp.where(eight, tiles[i + 8], tiles[i]) if i < need else tiles[i]
                    for i in range(need + 7)
                ]
                step = [jnp.where(four, step[i + 4], step[i]) for i in range(need + 3)]
                step = [jnp.where(two, step[i + 2], step[i]) for i in range(need + 1)]
                for i in range(need):
                    window[part, i * 8 : i * 8 + 8, :] = jnp.where(one, step[i + 1], step[i])
                for i in range(count):
                    total = None
                    for m in range(TAPS):
                        term = taps[m] * window[part, i * 8 + 5 + m : i * 8 + 13 + m, :]
                        total = term if total is None else total + term
                    out_ref[part, pl.ds(base + i * 8, 8), pl.ds(pl.multiple_of(tile * LANES, LANES), LANES)] = total
            return carry

        lax.fori_loop(0, 4, body, 0)
        store(seg, first, count).start()

    def store(seg, first, count):
        rows = pl.ds(pl.multiple_of((seg * 16 + first) * 8, 8), count * 8)
        which = 2 * seg + (1 if first == EARLY else 0) if first + count > 1 else 2 * CHUNKS
        return pltpu.make_async_copy(
            out_ref.at[:, rows], out_hbm.at[:, rows], store_sem.at[which]
        )

    def halo(towards, source_row, target_row, count, which):
        return pltpu.make_async_remote_copy(
            src_ref=focus.at[:, pl.ds(source_row, count)],
            dst_ref=focus.at[:, pl.ds(target_row, count)],
            send_sem=halo_send.at[which],
            recv_sem=halo_recv.at[which],
            device_id=(me, towards),
            device_id_type=MESH,
        )

    to_down = halo(down, BEFORE, BEFORE + ROWS, AFTER, 0)
    to_up = halo(up, BEFORE + ROWS - 8, 0, 8, 1)

    focus_rows(0)
    to_down.start()
    stolt(0, 1, EARLY - 1)

    def middle(chunk, carry):
        focus_rows(chunk)
        stolt(chunk - 1, EARLY, 16 - EARLY)
        stolt(chunk, 0, EARLY)
        return carry

    lax.fori_loop(1, CHUNKS - 1, middle, 0)
    focus_rows(CHUNKS - 1)
    to_up.start()
    stolt(CHUNKS - 2, EARLY, 16 - EARLY)
    to_down.wait_recv()

    @pl.when(rg == N_RG - 1)
    def _():
        focus[:, pl.ds(BEFORE + ROWS, AFTER), :] = jnp.zeros((8, AFTER, LANES), jnp.float32)

    stolt(CHUNKS - 1, 0, EARLY)
    stolt(CHUNKS - 1, EARLY, 16 - EARLY)
    to_up.wait_recv()

    @pl.when(rg == 0)
    def _():
        focus[:, pl.ds(0, BEFORE), :] = jnp.zeros((8, BEFORE, LANES), jnp.float32)

    stolt(0, 0, 1)
    store(0, 0, 1).wait()
    store(0, 1, EARLY - 1).wait()
    store(0, EARLY, 16 - EARLY).wait()
    for seg in range(1, CHUNKS):
        store(seg, 0, EARLY).wait()
        store(seg, EARLY, 16 - EARLY).wait()
    to_down.wait_send()
    to_up.wait_send()
    for chunk in range(CHUNKS):
        all_of(out_flat, in_flat, send1, recv1, chunk).wait_send()
        all_of(spec_flat, back_flat, send2, recv2, chunk).wait_send()


def on_device(echo_data, chirp_phase, stolt_shift, tap_index):
    tables = [jnp.asarray(table) for table in dft_tables()]
    hbm_spec = pl.BlockSpec(memory_space=pltpu.HBM)
    f32 = jnp.float32
    return pl.pallas_call(
        kernel,
        out_shape=jax.ShapeDtypeStruct((2, ROWS, COLS), f32),
        in_specs=[hbm_spec] * 9,
        out_specs=hbm_spec,
        scratch_shapes=[
            pltpu.VMEM((2, ROWS, COLS), f32),
            pltpu.VMEM((2, ROWS, COLS), f32),
            pltpu.VMEM((ROWS // LANES, LANES), f32),
            pltpu.VMEM((CHUNKS, COLS), jnp.int32),
            pltpu.VMEM((CHUNKS, COLS), jnp.int32),
            pltpu.VMEM((512, 512), jnp.bfloat16),
            pltpu.VMEM((512, 512), jnp.bfloat16),
            pltpu.VMEM((256, 256), jnp.bfloat16),
            pltpu.VMEM((256, 256), jnp.bfloat16),
            pltpu.VMEM((2, FIRST, SECOND), f32),
            pltpu.VMEM((FLAT, LANES), f32),
            pltpu.VMEM((FLAT, LANES), f32),
            pltpu.VMEM((FLAT, LANES), f32),
            pltpu.VMEM((FLAT, LANES), f32),
            pltpu.VMEM((4, ROWS, LANES), f32),
            pltpu.VMEM((4, ROWS, LANES), f32),
            pltpu.VMEM((8, FOCUS_ROWS, LANES), f32),
            pltpu.VMEM((16, 16, LANES), f32),
            pltpu.VMEM((16, 8, LANES), jnp.int32),
            pltpu.VMEM((ROWS, LANES), f32),
            pltpu.VMEM((ROWS, LANES), f32),
            pltpu.VMEM((2, 160, LANES), f32),
            pltpu.SemaphoreType.DMA((CHUNKS,)),
            pltpu.SemaphoreType.DMA((8,)),
            pltpu.SemaphoreType.DMA((2 * CHUNKS + 1,)),
            pltpu.SemaphoreType.DMA((CHUNKS,)),
            pltpu.SemaphoreType.DMA((CHUNKS,)),
            pltpu.SemaphoreType.DMA((CHUNKS,)),
            pltpu.SemaphoreType.DMA((CHUNKS,)),
            pltpu.SemaphoreType.DMA((2,)),
            pltpu.SemaphoreType.DMA((2,)),
        ],
        compiler_params=pltpu.CompilerParams(
            collective_id=0, has_side_effects=True, vmem_limit_bytes=58 << 20
        ),
    )(echo_data, chirp_phase.reshape(ROWS // LANES, LANES), stolt_shift, tap_index, *tables)


def solution(mesh):
    return jax.shard_map(
        on_device,
        mesh=mesh,
        in_specs=(P(None, "rg", "az"), P("rg"), P("rg", "az"), P("rg", "az")),
        out_specs=P(None, "rg", "az"),
        check_vma=False,
    )
```

```python
import math

import jax
import jax.numpy as jnp
import numpy as np
from jax import lax
from jax.experimental import pallas as pl
from jax.experimental.pallas import tpu as pltpu
from jax.sharding import PartitionSpec as P

MESH = pl.DeviceIdType.MESH
N_AZ = 64
N_RG = 4
ROWS = 512
COLS = 512
FULL = N_AZ * COLS
LANES = 128
FIRST = 256
SECOND = 128
CHUNKS = 4
CHUNK_ROWS = ROWS // CHUNKS
PAIR = CHUNK_ROWS // N_AZ
BLOCK = PAIR * 8
CHUNK_FLAT = N_AZ * BLOCK
FLAT = CHUNKS * CHUNK_FLAT
BEFORE = 8
AFTER = 72
FOCUS_ROWS = BEFORE + ROWS + AFTER + 8
TAPS = 15
EARLY = 7


def split(array):
    high = array.astype(jnp.bfloat16)
    low = (array - np.asarray(high).astype(np.float64)).astype(jnp.bfloat16)
    return high, low


def dft_tables():
    a = np.arange(FIRST)
    angle = 2.0 * np.pi * (np.outer(a, a) % FIRST) / FIRST
    cosine = np.cos(angle).reshape(FIRST, N_AZ, 4)
    sine = np.sin(angle).reshape(FIRST, N_AZ, 4)
    first = np.stack(
        [np.stack([cosine, sine], axis=2), np.stack([-sine, cosine], axis=2)], axis=0
    ).reshape(2 * FIRST, N_AZ * 8)
    angle = 2.0 * np.pi * (np.outer(a, np.arange(SECOND)) % FULL) / FULL
    norm = 1.0 / math.sqrt(FULL)
    twiddle = np.stack([np.cos(angle), np.sin(angle)]) * norm
    b = np.arange(SECOND)
    angle = 2.0 * np.pi * (np.outer(b, b) % SECOND) / SECOND
    cosine = np.cos(angle).reshape(N_AZ, 2, SECOND).transpose(1, 0, 2)
    sine = np.sin(angle).reshape(N_AZ, 2, SECOND).transpose(1, 0, 2)
    second = np.stack(
        [np.concatenate([cosine, sine], axis=2), np.concatenate([-sine, cosine], axis=2)], axis=0
    ).reshape(2 * SECOND, 2 * SECOND)
    first_high, first_low = split(first)
    second_high, second_low = split(second)
    return first_high, first_low, second_high, second_low, twiddle.astype(np.float32)


def sin_cos_of(rest, count):
    sign = 1.0 - 2.0 * (count - 2.0 * jnp.floor(count * 0.5))
    square = rest * rest
    sine = -1.0 / math.factorial(11)
    for order in (9, 7, 5, 3, 1):
        sine = sine * square + (-1.0) ** (order // 2) / math.factorial(order)
    cosine = 1.0 / math.factorial(12)
    for order in (10, 8, 6, 4, 2, 0):
        cosine = cosine * square + (-1.0) ** (order // 2) / math.factorial(order)
    return sine * rest * sign, cosine * sign


def sin_cos(angle):
    count = jnp.floor(angle * (1.0 / math.pi) + 0.5)
    rest = (angle - count * 3.140625) - count * (math.pi - 3.140625)
    return sin_cos_of(rest, count)


def sin_cos_pi(turns):
    count = jnp.floor(turns + 0.5)
    return sin_cos_of((turns - count) * math.pi, count)


def dot3(table_high, table_low, value, contract_on):
    high = value.astype(jnp.bfloat16)
    low = (value - high.astype(jnp.float32)).astype(jnp.bfloat16)
    dims = (((1,), (contract_on,)), ((), ()))
    dot = lambda left, right: lax.dot_general(left, right, dims, preferred_element_type=jnp.float32)
    return dot(table_high, high) + (dot(table_high, low) + dot(table_low, high))


def kernel(
    echo_hbm, chirp_hbm, shift_hbm, tap_hbm, t1h_hbm, t1l_hbm, t2h_hbm, t2l_hbm, tw_hbm,
    out_hbm,
    out_ref, echo, chirp_ref, shift_ref, tap_ref, t1h, t1l, t2h, t2l, tw, out_flat, in_flat, spec_flat, back_flat, phase_cos, phase_sin,
    focus, weights, coarse, chirp_cos, chirp_sin, window,
    load_sem, table_sem, store_sem, send1, recv1, send2, recv2, halo_send, halo_recv,
):
    me = lax.axis_index("az")
    rg = lax.axis_index("rg")
    up = lax.rem(rg + 1, N_RG)
    down = lax.rem(rg + N_RG - 1, N_RG)

    barrier = pltpu.get_barrier_semaphore()

    def greet(i, carry):
        pl.semaphore_signal(
            barrier, inc=1, device_id=(lax.rem(me + i, N_AZ), rg), device_id_type=MESH
        )
        return carry

    chirp_copy = pltpu.make_async_copy(chirp_hbm, chirp_ref, table_sem.at[5])
    chirp_copy.start()
    echo_copies = []
    for chunk in range(CHUNKS):
        rows = pl.ds(chunk * CHUNK_ROWS, CHUNK_ROWS)
        echo_copies.append(
            pltpu.make_async_copy(echo_hbm.at[:, rows], echo.at[:, rows], load_sem.at[chunk])
        )
        echo_copies[-1].start()
    lax.fori_loop(1, N_AZ, greet, 0)
    for other in (up, down):
        pl.semaphore_signal(barrier, inc=1, device_id=(me, other), device_id_type=MESH)
    table_copies = []
    for index, (source, target) in enumerate(
        (
            (t1h_hbm, t1h), (t1l_hbm, t1l), (t2h_hbm, t2h), (t2l_hbm, t2l), (tw_hbm, tw),
        )
    ):
        table_copies.append(pltpu.make_async_copy(source, target, table_sem.at[index]))
        table_copies[-1].start()

    shift_copy = pltpu.make_async_copy(shift_hbm, shift_ref, table_sem.at[6])
    tap_copy = pltpu.make_async_copy(tap_hbm, tap_ref, table_sem.at[7])
    shift_copy.start()
    tap_copy.start()

    chirp_copy.wait()
    sine, cosine = sin_cos_pi(chirp_ref[...] * (1.0 / math.pi))
    for part in range(ROWS // LANES):
        rows = pl.ds(part * LANES, LANES)
        chirp_cos[rows, :] = jnp.transpose(
            jnp.broadcast_to(cosine[part : part + 1, :], (LANES, LANES))
        )
        chirp_sin[rows, :] = jnp.transpose(
            jnp.broadcast_to(sine[part : part + 1, :], (LANES, LANES))
        )

    def matched(chunk):
        def body(i, carry):
            row = pl.multiple_of(chunk * CHUNK_ROWS + i * 8, 8)
            c = chirp_cos[pl.ds(row, 8), :]
            s = chirp_sin[pl.ds(row, 8), :]
            for tile in range(4):
                lanes = slice(tile * LANES, (tile + 1) * LANES)
                re = echo[0, pl.ds(row, 8), lanes]
                im = echo[1, pl.ds(row, 8), lanes]
                out_flat[pl.ds(row * 8 + tile, 8, stride=8), :] = re * c + im * s
                out_flat[pl.ds(row * 8 + 4 + tile, 8, stride=8), :] = im * c - re * s
            return carry

        lax.fori_loop(0, CHUNK_ROWS // 8, body, 0)

    def exchange(source, target, send, recv, chunk, beside=None):
        def body(i, carry):
            other = lax.rem(me + i, N_AZ)
            away = pl.multiple_of(chunk * CHUNK_FLAT + other * BLOCK, BLOCK)
            home = pl.multiple_of(chunk * CHUNK_FLAT + me * BLOCK, BLOCK)
            pltpu.make_async_remote_copy(
                src_ref=source.at[pl.ds(away, BLOCK)],
                dst_ref=target.at[pl.ds(home, BLOCK)],
                send_sem=send.at[chunk],
                recv_sem=recv.at[chunk],
                device_id=(other, rg),
                device_id_type=MESH,
            ).start()
            if beside is not None:
                beside(i - 1)
            return carry

        lax.fori_loop(1, N_AZ, body, 0)
        home = pl.multiple_of(chunk * CHUNK_FLAT + me * BLOCK, BLOCK)
        target[pl.ds(home, BLOCK), :] = source[pl.ds(home, BLOCK), :]

    def all_of(source, target, send, recv, chunk):
        rows = pl.ds(pl.multiple_of(chunk * CHUNK_FLAT, BLOCK), CHUNK_FLAT - BLOCK)
        return pltpu.make_async_remote_copy(
            src_ref=source.at[rows],
            dst_ref=target.at[rows],
            send_sem=send.at[chunk],
            recv_sem=recv.at[chunk],
            device_id=(lax.rem(me + 1, N_AZ), rg),
            device_id_type=MESH,
        )

    echo_copies[0].wait()
    matched(0)
    pl.semaphore_wait(barrier, N_AZ + 1)
    exchange(out_flat, in_flat, send1, recv1, 0)
    echo_copies[3].wait()
    matched(3)
    exchange(out_flat, in_flat, send1, recv1, 3)
    for chunk in (2, 1):
        echo_copies[chunk].wait()
        matched(chunk)

    lane_id = lax.broadcasted_iota(jnp.int32, (8, LANES), 1)
    row_id = lax.broadcasted_iota(jnp.int32, (8, LANES), 0)

    def phase_body(i, carry):
        row = pl.multiple_of(i * 8, 8)
        r = 1.0 + (rg * ROWS + row + row_id).astype(jnp.float32) * (1.0 / (ROWS * N_RG))
        rr = r * r
        for tile in range(4):
            line = me * COLS + tile * LANES + lane_id
            signed = jnp.where(line < FULL // 2, line, line - FULL)
            q = signed.astype(jnp.float32) * (0.9 / (FULL // 2))
            s, c = sin_cos(40.0 * jnp.sqrt(rr - q * q))
            phase_cos[tile, pl.ds(row, 8), :] = c
            phase_sin[tile, pl.ds(row, 8), :] = s
        return carry

    lax.fori_loop(0, ROWS // 8, phase_body, 0)

    shift_copy.wait()
    tap_copy.wait()
    tap_id = lax.broadcasted_iota(jnp.int32, (16, LANES), 0)
    for seg in range(CHUNKS):
        for tile in range(4):
            lanes = slice(tile * LANES, (tile + 1) * LANES)
            shift = shift_ref[seg : seg + 1, lanes]
            slot = tap_id - jnp.broadcast_to(shift & 7, (16, LANES))
            frac = jnp.broadcast_to(tap_ref[seg : seg + 1, lanes], (16, LANES))
            u = (slot - 3).astype(jnp.float32) - frac.astype(jnp.float32) * (1.0 / 16.0)
            sine, _ = sin_cos_pi(u)
            _, cosine = sin_cos_pi(u * 0.25)
            at_zero = u == 0.0
            sinc = jnp.where(at_zero, 1.0, sine / jnp.where(at_zero, 1.0, u * math.pi))
            inside = jnp.logical_and(slot >= 0, slot < 8)
            weights[seg * 4 + tile] = jnp.where(inside, sinc * (0.54 + 0.46 * cosine), 0.0)
            coarse[seg * 4 + tile] = jnp.broadcast_to(shift >> 3, (8, LANES))

    for plane in range(8):
        focus[plane, pl.ds(BEFORE, ROWS), :] = jnp.zeros((ROWS, LANES), jnp.float32)
        focus[plane, pl.ds(BEFORE + ROWS + AFTER, 8), :] = jnp.zeros((8, LANES), jnp.float32)

    for copy in table_copies:
        copy.wait()

    def transform(chunk):
        all_of(out_flat, in_flat, send1, recv1, chunk).wait_recv()
        start = pl.multiple_of(chunk * CHUNK_FLAT, CHUNK_FLAT)
        both = in_flat[pl.ds(start, CHUNK_FLAT), :].reshape(N_AZ, PAIR, 8, LANES)
        signal = jnp.concatenate(
            [both[:, pair].reshape(N_AZ * 8, LANES) for pair in range(PAIR)], axis=1
        )
        section = dot3(t1h[...], t1l[...], signal, 0)
        for pair in range(PAIR):
            lanes = slice(pair * LANES, (pair + 1) * LANES)
            re = section[:FIRST, lanes]
            im = section[FIRST:, lanes]
            turned = jnp.concatenate([re * tw[0] + im * tw[1], im * tw[0] - re * tw[1]], axis=1)
            final = dot3(t2h[...], t2l[...], turned, 1)
            for quarter in range(4):
                for half in range(2):
                    spec_flat[pl.ds(start + pair * 8 + quarter * 2 + half, N_AZ, stride=BLOCK), :] = (
                        final[quarter * N_AZ : (quarter + 1) * N_AZ, half * LANES : (half + 1) * LANES]
                    )
        exchange(spec_flat, back_flat, send2, recv2, chunk)

    def focus_rows(chunk):
        all_of(spec_flat, back_flat, send2, recv2, chunk).wait_recv()

        def body(i, carry):
            row = pl.multiple_of(chunk * CHUNK_ROWS + i * 8, 8)
            for tile in range(4):
                a = back_flat[pl.ds(row * 8 + tile, 8, stride=8), :]
                b = back_flat[pl.ds(row * 8 + 4 + tile, 8, stride=8), :]
                c = phase_cos[tile, pl.ds(row, 8), :]
                s = phase_sin[tile, pl.ds(row, 8), :]
                focus[tile, pl.ds(BEFORE + row, 8), :] = a * c - b * s
                focus[4 + tile, pl.ds(BEFORE + row, 8), :] = a * s + b * c
            return carry

        lax.fori_loop(0, CHUNK_ROWS // 8, body, 0)

    def stolt(seg, first, count):
        def body(tile, carry):
            index = seg * 4 + tile
            h = coarse[index]
            eight = h >= 8
            four = (h & 4) != 0
            two = (h & 2) != 0
            one = (h & 1) != 0
            taps = [jnp.broadcast_to(weights[index, m : m + 1, :], (8, LANES)) for m in range(TAPS)]
            for part in range(2):
                plane = part * 4 + tile
                need = count + 3
                base = pl.multiple_of((seg * 16 + first) * 8, 8)
                load = lambda i: focus[plane, pl.ds(base + i * 8, 8), :]
                tiles = [load(i) for i in range(need + 8)]
                step = [
                    jnp.where(eight, tiles[i + 8], tiles[i]) if i < need else tiles[i]
                    for i in range(need + 7)
                ]
                step = [jnp.where(four, step[i + 4], step[i]) for i in range(need + 3)]
                step = [jnp.where(two, step[i + 2], step[i]) for i in range(need + 1)]
                for i in range(need):
                    window[part, i * 8 : i * 8 + 8, :] = jnp.where(one, step[i + 1], step[i])
                for i in range(count):
                    total = None
                    for m in range(TAPS):
                        term = taps[m] * window[part, i * 8 + 5 + m : i * 8 + 13 + m, :]
                        total = term if total is None else total + term
                    out_ref[part, pl.ds(base + i * 8, 8), pl.ds(pl.multiple_of(tile * LANES, LANES), LANES)] = total
            return carry

        lax.fori_loop(0, 4, body, 0)
        store(seg, first, count).start()

    def store(seg, first, count):
        rows = pl.ds(pl.multiple_of((seg * 16 + first) * 8, 8), count * 8)
        which = 2 * seg + (1 if first == EARLY else 0) if count > 1 else 2 * CHUNKS + seg - 2
        return pltpu.make_async_copy(
            out_ref.at[:, rows], out_hbm.at[:, rows], store_sem.at[which]
        )

    def halo(towards, source_row, target_row, which):
        def piece(plane, start, count):
            return pltpu.make_async_remote_copy(
                src_ref=focus.at[plane, pl.ds(source_row + start, count)],
                dst_ref=focus.at[plane, pl.ds(target_row + start, count)],
                send_sem=halo_send.at[which],
                recv_sem=halo_recv.at[which],
                device_id=(me, towards),
                device_id_type=MESH,
            )

        return piece

    down_piece = halo(down, BEFORE, BEFORE + ROWS, 0)
    up_piece = halo(up, BEFORE + ROWS - BEFORE, 0, 1)
    to_down = down_piece(slice(None), 0, AFTER)
    to_up = up_piece(slice(None), 0, BEFORE)

    def send_down(piece):
        down_piece(piece // 9, pl.multiple_of(piece % 9 * 8, 8), 8).start()

    def step(k, carry):
        now = (CHUNKS - k) % CHUNKS
        transform(now)

        @pl.when(k == 0)
        def _():
            exchange(out_flat, in_flat, send1, recv1, 2)

        @pl.when(k >= 1)
        def _():
            focus_rows((CHUNKS + 1 - k) % CHUNKS)

        @pl.when(k == 1)
        def _():
            exchange(out_flat, in_flat, send1, recv1, 1, beside=send_down)
            for piece in range(N_AZ - 1, 72):
                send_down(piece)

        @pl.when(k == 2)
        def _():
            for plane in range(8):
                up_piece(plane, 0, BEFORE).start()
            to_down.wait_recv()

            @pl.when(rg == N_RG - 1)
            def _():
                focus[:, pl.ds(BEFORE + ROWS, AFTER), :] = jnp.zeros((8, AFTER, LANES), jnp.float32)

        @pl.when(k >= 2)
        def _():
            seg = CHUNKS + 1 - k
            stolt(seg, 1, EARLY - 1)
            stolt(seg, EARLY, 16 - EARLY)

        return carry

    lax.fori_loop(0, CHUNKS, step, 0)
    stolt(3, 0, 1)
    to_up.wait_recv()

    @pl.when(rg == 0)
    def _():
        focus[:, pl.ds(0, BEFORE), :] = jnp.zeros((8, BEFORE, LANES), jnp.float32)

    stolt(0, 0, EARLY)
    focus_rows(1)
    stolt(0, EARLY, 16 - EARLY)
    stolt(1, 0, EARLY)
    stolt(1, EARLY, 16 - EARLY)
    stolt(2, 0, 1)
    for seg in range(CHUNKS):
        if seg < 2:
            store(seg, 0, EARLY).wait()
        else:
            store(seg, 0, 1).wait()
            store(seg, 1, EARLY - 1).wait()
        store(seg, EARLY, 16 - EARLY).wait()
    to_down.wait_send()
    to_up.wait_send()
    for chunk in range(CHUNKS):
        all_of(out_flat, in_flat, send1, recv1, chunk).wait_send()
        all_of(spec_flat, back_flat, send2, recv2, chunk).wait_send()


def on_device(echo_data, chirp_phase, stolt_shift, tap_index):
    tables = [jnp.asarray(table) for table in dft_tables()]
    hbm_spec = pl.BlockSpec(memory_space=pltpu.HBM)
    f32 = jnp.float32
    return pl.pallas_call(
        kernel,
        out_shape=jax.ShapeDtypeStruct((2, ROWS, COLS), f32),
        in_specs=[hbm_spec] * 9,
        out_specs=hbm_spec,
        scratch_shapes=[
            pltpu.VMEM((2, ROWS, COLS), f32),
            pltpu.VMEM((2, ROWS, COLS), f32),
            pltpu.VMEM((ROWS // LANES, LANES), f32),
            pltpu.VMEM((CHUNKS, COLS), jnp.int32),
            pltpu.VMEM((CHUNKS, COLS), jnp.int32),
            pltpu.VMEM((512, 512), jnp.bfloat16),
            pltpu.VMEM((512, 512), jnp.bfloat16),
            pltpu.VMEM((256, 256), jnp.bfloat16),
            pltpu.VMEM((256, 256), jnp.bfloat16),
            pltpu.VMEM((2, FIRST, SECOND), f32),
            pltpu.VMEM((FLAT, LANES), f32),
            pltpu.VMEM((FLAT, LANES), f32),
            pltpu.VMEM((FLAT, LANES), f32),
            pltpu.VMEM((FLAT, LANES), f32),
            pltpu.VMEM((4, ROWS, LANES), f32),
            pltpu.VMEM((4, ROWS, LANES), f32),
            pltpu.VMEM((8, FOCUS_ROWS, LANES), f32),
            pltpu.VMEM((16, 16, LANES), f32),
            pltpu.VMEM((16, 8, LANES), jnp.int32),
            pltpu.VMEM((ROWS, LANES), f32),
            pltpu.VMEM((ROWS, LANES), f32),
            pltpu.VMEM((2, 160, LANES), f32),
            pltpu.SemaphoreType.DMA((CHUNKS,)),
            pltpu.SemaphoreType.DMA((8,)),
            pltpu.SemaphoreType.DMA((2 * CHUNKS + 2,)),
            pltpu.SemaphoreType.DMA((CHUNKS,)),
            pltpu.SemaphoreType.DMA((CHUNKS,)),
            pltpu.SemaphoreType.DMA((CHUNKS,)),
            pltpu.SemaphoreType.DMA((CHUNKS,)),
            pltpu.SemaphoreType.DMA((2,)),
            pltpu.SemaphoreType.DMA((2,)),
        ],
        compiler_params=pltpu.CompilerParams(
            collective_id=0, has_side_effects=True, vmem_limit_bytes=58 << 20
        ),
    )(echo_data, chirp_phase.reshape(ROWS // LANES, LANES), stolt_shift, tap_index, *tables)


def solution(mesh):
    return jax.shard_map(
        on_device,
        mesh=mesh,
        in_specs=(P(None, "rg", "az"), P("rg"), P("rg", "az"), P("rg", "az")),
        out_specs=P(None, "rg", "az"),
        check_vma=False,
    )
```

```python
import math

import jax
import jax.numpy as jnp
import numpy as np
from jax import lax
from jax.experimental import pallas as pl
from jax.experimental.pallas import tpu as pltpu
from jax.sharding import PartitionSpec as P

MESH = pl.DeviceIdType.MESH
N_AZ = 64
N_RG = 4
ROWS = 512
COLS = 512
FULL = N_AZ * COLS
LANES = 128
FIRST = 256
SECOND = 128
CHUNKS = 4
CHUNK_ROWS = ROWS // CHUNKS
PAIR = CHUNK_ROWS // N_AZ
BLOCK = PAIR * 8
CHUNK_FLAT = N_AZ * BLOCK
FLAT = CHUNKS * CHUNK_FLAT
BEFORE = 8
AFTER = 72
FOCUS_ROWS = BEFORE + ROWS + AFTER + 8
TAPS = 15
EARLY = 7


def split(array):
    high = array.astype(jnp.bfloat16)
    low = (array - np.asarray(high).astype(np.float64)).astype(jnp.bfloat16)
    return high, low


def dft_tables():
    a = np.arange(FIRST)
    angle = 2.0 * np.pi * (np.outer(a, a) % FIRST) / FIRST
    cosine = np.cos(angle).reshape(FIRST, N_AZ, 4)
    sine = np.sin(angle).reshape(FIRST, N_AZ, 4)
    first = np.stack(
        [np.stack([cosine, sine], axis=2), np.stack([-sine, cosine], axis=2)], axis=0
    ).reshape(2 * FIRST, N_AZ * 8)
    angle = 2.0 * np.pi * (np.outer(a, np.arange(SECOND)) % FULL) / FULL
    norm = 1.0 / math.sqrt(FULL)
    twiddle = np.stack([np.cos(angle), np.sin(angle)]) * norm
    b = np.arange(SECOND)
    angle = 2.0 * np.pi * (np.outer(b, b) % SECOND) / SECOND
    cosine = np.cos(angle).reshape(N_AZ, 2, SECOND).transpose(1, 0, 2)
    sine = np.sin(angle).reshape(N_AZ, 2, SECOND).transpose(1, 0, 2)
    second = np.stack(
        [np.concatenate([cosine, sine], axis=2), np.concatenate([-sine, cosine], axis=2)], axis=0
    ).reshape(2 * SECOND, 2 * SECOND)
    first_high, first_low = split(first)
    second_high, second_low = split(second)
    return first_high, first_low, second_high, second_low, twiddle.astype(np.float32)


def sin_cos_of(rest, count):
    sign = 1.0 - 2.0 * (count - 2.0 * jnp.floor(count * 0.5))
    square = rest * rest
    sine = -1.0 / math.factorial(11)
    for order in (9, 7, 5, 3, 1):
        sine = sine * square + (-1.0) ** (order // 2) / math.factorial(order)
    cosine = 1.0 / math.factorial(12)
    for order in (10, 8, 6, 4, 2, 0):
        cosine = cosine * square + (-1.0) ** (order // 2) / math.factorial(order)
    return sine * rest * sign, cosine * sign


def sin_cos(angle):
    count = jnp.floor(angle * (1.0 / math.pi) + 0.5)
    rest = (angle - count * 3.140625) - count * (math.pi - 3.140625)
    return sin_cos_of(rest, count)


def sin_cos_pi(turns):
    count = jnp.floor(turns + 0.5)
    return sin_cos_of((turns - count) * math.pi, count)


def dot3(table_high, table_low, value, contract_on):
    high = value.astype(jnp.bfloat16)
    low = (value - high.astype(jnp.float32)).astype(jnp.bfloat16)
    dims = (((1,), (contract_on,)), ((), ()))
    dot = lambda left, right: lax.dot_general(left, right, dims, preferred_element_type=jnp.float32)
    return dot(table_high, high) + (dot(table_high, low) + dot(table_low, high))


def kernel(
    echo_hbm, chirp_hbm, shift_hbm, tap_hbm, t1h_hbm, t1l_hbm, t2h_hbm, t2l_hbm, tw_hbm,
    out_ref,
    echo, chirp_ref, shift_ref, tap_ref, t1h, t1l, t2h, t2l, tw, out_flat, in_flat, spec_flat, back_flat, phase_cos, phase_sin,
    focus, weights, coarse, chirp_cos, chirp_sin, window,
    load_sem, table_sem, send1, recv1, send2, recv2, halo_send, halo_recv,
):
    me = lax.axis_index("az")
    rg = lax.axis_index("rg")
    up = lax.rem(rg + 1, N_RG)
    down = lax.rem(rg + N_RG - 1, N_RG)

    barrier = pltpu.get_barrier_semaphore()

    def greet(i, carry):
        pl.semaphore_signal(
            barrier, inc=1, device_id=(lax.rem(me + i, N_AZ), rg), device_id_type=MESH
        )
        return carry

    chirp_copy = pltpu.make_async_copy(chirp_hbm, chirp_ref, table_sem.at[5])
    chirp_copy.start()
    echo_copies = []
    for chunk in range(CHUNKS):
        rows = pl.ds(chunk * CHUNK_ROWS, CHUNK_ROWS)
        echo_copies.append(
            pltpu.make_async_copy(echo_hbm.at[:, rows], echo.at[:, rows], load_sem.at[chunk])
        )
        echo_copies[-1].start()
    lax.fori_loop(1, N_AZ, greet, 0)
    for other in (up, down):
        pl.semaphore_signal(barrier, inc=1, device_id=(me, other), device_id_type=MESH)
    table_copies = []
    for index, (source, target) in enumerate(
        (
            (t1h_hbm, t1h), (t1l_hbm, t1l), (t2h_hbm, t2h), (t2l_hbm, t2l), (tw_hbm, tw),
        )
    ):
        table_copies.append(pltpu.make_async_copy(source, target, table_sem.at[index]))
        table_copies[-1].start()

    shift_copy = pltpu.make_async_copy(shift_hbm, shift_ref, table_sem.at[6])
    tap_copy = pltpu.make_async_copy(tap_hbm, tap_ref, table_sem.at[7])
    shift_copy.start()
    tap_copy.start()

    chirp_copy.wait()
    sine, cosine = sin_cos_pi(chirp_ref[...] * (1.0 / math.pi))
    for part in range(ROWS // LANES):
        rows = pl.ds(part * LANES, LANES)
        chirp_cos[rows, :] = jnp.transpose(
            jnp.broadcast_to(cosine[part : part + 1, :], (LANES, LANES))
        )
        chirp_sin[rows, :] = jnp.transpose(
            jnp.broadcast_to(sine[part : part + 1, :], (LANES, LANES))
        )

    def matched(chunk):
        def body(i, carry):
            row = pl.multiple_of(chunk * CHUNK_ROWS + i * 8, 8)
            c = chirp_cos[pl.ds(row, 8), :]
            s = chirp_sin[pl.ds(row, 8), :]
            for tile in range(4):
                lanes = slice(tile * LANES, (tile + 1) * LANES)
                re = echo[0, pl.ds(row, 8), lanes]
                im = echo[1, pl.ds(row, 8), lanes]
                out_flat[pl.ds(row * 8 + tile, 8, stride=8), :] = re * c + im * s
                out_flat[pl.ds(row * 8 + 4 + tile, 8, stride=8), :] = im * c - re * s
            return carry

        lax.fori_loop(0, CHUNK_ROWS // 8, body, 0)

    def exchange(source, target, send, recv, chunk, beside=None):
        def body(i, carry):
            other = lax.rem(me + i, N_AZ)
            away = pl.multiple_of(chunk * CHUNK_FLAT + other * BLOCK, BLOCK)
            home = pl.multiple_of(chunk * CHUNK_FLAT + me * BLOCK, BLOCK)
            pltpu.make_async_remote_copy(
                src_ref=source.at[pl.ds(away, BLOCK)],
                dst_ref=target.at[pl.ds(home, BLOCK)],
                send_sem=send.at[chunk],
                recv_sem=recv.at[chunk],
                device_id=(other, rg),
                device_id_type=MESH,
            ).start()
            if beside is not None:
                beside(i - 1)
            return carry

        lax.fori_loop(1, N_AZ, body, 0)
        home = pl.multiple_of(chunk * CHUNK_FLAT + me * BLOCK, BLOCK)
        target[pl.ds(home, BLOCK), :] = source[pl.ds(home, BLOCK), :]

    def all_of(source, target, send, recv, chunk):
        rows = pl.ds(pl.multiple_of(chunk * CHUNK_FLAT, BLOCK), CHUNK_FLAT - BLOCK)
        return pltpu.make_async_remote_copy(
            src_ref=source.at[rows],
            dst_ref=target.at[rows],
            send_sem=send.at[chunk],
            recv_sem=recv.at[chunk],
            device_id=(lax.rem(me + 1, N_AZ), rg),
            device_id_type=MESH,
        )

    echo_copies[0].wait()
    matched(0)
    pl.semaphore_wait(barrier, N_AZ + 1)
    exchange(out_flat, in_flat, send1, recv1, 0)
    echo_copies[3].wait()
    matched(3)
    exchange(out_flat, in_flat, send1, recv1, 3)
    for chunk in (2, 1):
        echo_copies[chunk].wait()
        matched(chunk)

    lane_id = lax.broadcasted_iota(jnp.int32, (8, LANES), 1)
    row_id = lax.broadcasted_iota(jnp.int32, (8, LANES), 0)

    def phase_body(i, carry):
        row = pl.multiple_of(i * 8, 8)
        r = 1.0 + (rg * ROWS + row + row_id).astype(jnp.float32) * (1.0 / (ROWS * N_RG))
        rr = r * r
        for tile in range(4):
            line = me * COLS + tile * LANES + lane_id
            signed = jnp.where(line < FULL // 2, line, line - FULL)
            q = signed.astype(jnp.float32) * (0.9 / (FULL // 2))
            s, c = sin_cos(40.0 * jnp.sqrt(rr - q * q))
            phase_cos[tile, pl.ds(row, 8), :] = c
            phase_sin[tile, pl.ds(row, 8), :] = s
        return carry

    lax.fori_loop(0, ROWS // 8, phase_body, 0)

    shift_copy.wait()
    tap_copy.wait()
    tap_id = lax.broadcasted_iota(jnp.int32, (16, LANES), 0)
    for seg in range(CHUNKS):
        for tile in range(4):
            lanes = slice(tile * LANES, (tile + 1) * LANES)
            shift = shift_ref[seg : seg + 1, lanes]
            slot = tap_id - jnp.broadcast_to(shift & 7, (16, LANES))
            frac = jnp.broadcast_to(tap_ref[seg : seg + 1, lanes], (16, LANES))
            u = (slot - 3).astype(jnp.float32) - frac.astype(jnp.float32) * (1.0 / 16.0)
            sine, _ = sin_cos_pi(u)
            _, cosine = sin_cos_pi(u * 0.25)
            at_zero = u == 0.0
            sinc = jnp.where(at_zero, 1.0, sine / jnp.where(at_zero, 1.0, u * math.pi))
            inside = jnp.logical_and(slot >= 0, slot < 8)
            weights[seg * 4 + tile] = jnp.where(inside, sinc * (0.54 + 0.46 * cosine), 0.0)
            coarse[seg * 4 + tile] = jnp.broadcast_to(shift >> 3, (8, LANES))

    for plane in range(8):
        focus[plane, pl.ds(BEFORE, ROWS), :] = jnp.zeros((ROWS, LANES), jnp.float32)
        focus[plane, pl.ds(BEFORE + ROWS + AFTER, 8), :] = jnp.zeros((8, LANES), jnp.float32)

    for copy in table_copies:
        copy.wait()

    def transform(chunk):
        all_of(out_flat, in_flat, send1, recv1, chunk).wait_recv()
        start = pl.multiple_of(chunk * CHUNK_FLAT, CHUNK_FLAT)
        both = in_flat[pl.ds(start, CHUNK_FLAT), :].reshape(N_AZ, PAIR, 8, LANES)
        signal = jnp.concatenate(
            [both[:, pair].reshape(N_AZ * 8, LANES) for pair in range(PAIR)], axis=1
        )
        section = dot3(t1h[...], t1l[...], signal, 0)
        for pair in range(PAIR):
            lanes = slice(pair * LANES, (pair + 1) * LANES)
            re = section[:FIRST, lanes]
            im = section[FIRST:, lanes]
            turned = jnp.concatenate([re * tw[0] + im * tw[1], im * tw[0] - re * tw[1]], axis=1)
            final = dot3(t2h[...], t2l[...], turned, 1)
            for quarter in range(4):
                for half in range(2):
                    spec_flat[pl.ds(start + pair * 8 + quarter * 2 + half, N_AZ, stride=BLOCK), :] = (
                        final[quarter * N_AZ : (quarter + 1) * N_AZ, half * LANES : (half + 1) * LANES]
                    )
        exchange(spec_flat, back_flat, send2, recv2, chunk)

    def focus_rows(chunk):
        all_of(spec_flat, back_flat, send2, recv2, chunk).wait_recv()

        def body(i, carry):
            row = pl.multiple_of(chunk * CHUNK_ROWS + i * 8, 8)
            for tile in range(4):
                a = back_flat[pl.ds(row * 8 + tile, 8, stride=8), :]
                b = back_flat[pl.ds(row * 8 + 4 + tile, 8, stride=8), :]
                c = phase_cos[tile, pl.ds(row, 8), :]
                s = phase_sin[tile, pl.ds(row, 8), :]
                focus[tile, pl.ds(BEFORE + row, 8), :] = a * c - b * s
                focus[4 + tile, pl.ds(BEFORE + row, 8), :] = a * s + b * c
            return carry

        lax.fori_loop(0, CHUNK_ROWS // 8, body, 0)

    def stolt(seg, first, count):
        def body(tile, carry):
            index = seg * 4 + tile
            h = coarse[index]
            eight = h >= 8
            four = (h & 4) != 0
            two = (h & 2) != 0
            one = (h & 1) != 0
            taps = [jnp.broadcast_to(weights[index, m : m + 1, :], (8, LANES)) for m in range(TAPS)]
            for part in range(2):
                plane = part * 4 + tile
                need = count + 3
                base = pl.multiple_of((seg * 16 + first) * 8, 8)
                load = lambda i: focus[plane, pl.ds(base + i * 8, 8), :]
                tiles = [load(i) for i in range(need + 8)]
                step = [
                    jnp.where(eight, tiles[i + 8], tiles[i]) if i < need else tiles[i]
                    for i in range(need + 7)
                ]
                step = [jnp.where(four, step[i + 4], step[i]) for i in range(need + 3)]
                step = [jnp.where(two, step[i + 2], step[i]) for i in range(need + 1)]
                for i in range(need):
                    window[part, i * 8 : i * 8 + 8, :] = jnp.where(one, step[i + 1], step[i])
                for i in range(count):
                    total = None
                    for m in range(TAPS):
                        term = taps[m] * window[part, i * 8 + 5 + m : i * 8 + 13 + m, :]
                        total = term if total is None else total + term
                    out_ref[part, pl.ds(base + i * 8, 8), pl.ds(pl.multiple_of(tile * LANES, LANES), LANES)] = total
            return carry

        lax.fori_loop(0, 4, body, 0)

    def halo(towards, source_row, target_row, which):
        def piece(plane, start, count):
            return pltpu.make_async_remote_copy(
                src_ref=focus.at[plane, pl.ds(source_row + start, count)],
                dst_ref=focus.at[plane, pl.ds(target_row + start, count)],
                send_sem=halo_send.at[which],
                recv_sem=halo_recv.at[which],
                device_id=(me, towards),
                device_id_type=MESH,
            )

        return piece

    down_piece = halo(down, BEFORE, BEFORE + ROWS, 0)
    up_piece = halo(up, BEFORE + ROWS - BEFORE, 0, 1)
    to_down = down_piece(slice(None), 0, AFTER)
    to_up = up_piece(slice(None), 0, BEFORE)

    def send_down(piece):
        down_piece(piece // 9, pl.multiple_of(piece % 9 * 8, 8), 8).start()

    def step(k, carry):
        now = (CHUNKS - k) % CHUNKS
        transform(now)

        @pl.when(k == 0)
        def _():
            exchange(out_flat, in_flat, send1, recv1, 2)

        @pl.when(k >= 1)
        def _():
            focus_rows((CHUNKS + 1 - k) % CHUNKS)

        @pl.when(k == 1)
        def _():
            exchange(out_flat, in_flat, send1, recv1, 1, beside=send_down)
            for piece in range(N_AZ - 1, 72):
                send_down(piece)

        @pl.when(k == 2)
        def _():
            for plane in range(8):
                up_piece(plane, 0, BEFORE).start()
            to_down.wait_recv()

            @pl.when(rg == N_RG - 1)
            def _():
                focus[:, pl.ds(BEFORE + ROWS, AFTER), :] = jnp.zeros((8, AFTER, LANES), jnp.float32)

        @pl.when(k >= 2)
        def _():
            seg = CHUNKS + 1 - k
            stolt(seg, 1, EARLY - 1)
            stolt(seg, EARLY, 16 - EARLY)

        return carry

    lax.fori_loop(0, CHUNKS, step, 0)
    stolt(3, 0, 1)
    to_up.wait_recv()

    @pl.when(rg == 0)
    def _():
        focus[:, pl.ds(0, BEFORE), :] = jnp.zeros((8, BEFORE, LANES), jnp.float32)

    stolt(0, 0, EARLY)
    focus_rows(1)
    stolt(0, EARLY, 16 - EARLY)
    stolt(1, 0, EARLY)
    stolt(1, EARLY, 16 - EARLY)
    stolt(2, 0, 1)
    to_down.wait_send()
    to_up.wait_send()
    for chunk in range(CHUNKS):
        all_of(out_flat, in_flat, send1, recv1, chunk).wait_send()
        all_of(spec_flat, back_flat, send2, recv2, chunk).wait_send()


def on_device(echo_data, chirp_phase, stolt_shift, tap_index):
    tables = [jnp.asarray(table) for table in dft_tables()]
    hbm_spec = pl.BlockSpec(memory_space=pltpu.HBM)
    f32 = jnp.float32
    chirp = chirp_phase.reshape(ROWS // LANES, LANES)
    operands = [
        pltpu.with_memory_space_constraint(operand, pltpu.HBM)
        for operand in (echo_data, chirp, stolt_shift, tap_index, *tables)
    ]
    return pl.pallas_call(
        kernel,
        out_shape=pltpu.VMEM((2, ROWS, COLS), f32),
        in_specs=[hbm_spec] * 9,
        out_specs=pl.BlockSpec(memory_space=pltpu.VMEM),
        scratch_shapes=[
            pltpu.VMEM((2, ROWS, COLS), f32),
            pltpu.VMEM((ROWS // LANES, LANES), f32),
            pltpu.VMEM((CHUNKS, COLS), jnp.int32),
            pltpu.VMEM((CHUNKS, COLS), jnp.int32),
            pltpu.VMEM((512, 512), jnp.bfloat16),
            pltpu.VMEM((512, 512), jnp.bfloat16),
            pltpu.VMEM((256, 256), jnp.bfloat16),
            pltpu.VMEM((256, 256), jnp.bfloat16),
            pltpu.VMEM((2, FIRST, SECOND), f32),
            pltpu.VMEM((FLAT, LANES), f32),
            pltpu.VMEM((FLAT, LANES), f32),
            pltpu.VMEM((FLAT, LANES), f32),
            pltpu.VMEM((FLAT, LANES), f32),
            pltpu.VMEM((4, ROWS, LANES), f32),
            pltpu.VMEM((4, ROWS, LANES), f32),
            pltpu.VMEM((8, FOCUS_ROWS, LANES), f32),
            pltpu.VMEM((16, 16, LANES), f32),
            pltpu.VMEM((16, 8, LANES), jnp.int32),
            pltpu.VMEM((ROWS, LANES), f32),
            pltpu.VMEM((ROWS, LANES), f32),
            pltpu.VMEM((2, 160, LANES), f32),
            pltpu.SemaphoreType.DMA((CHUNKS,)),
            pltpu.SemaphoreType.DMA((8,)),
            pltpu.SemaphoreType.DMA((CHUNKS,)),
            pltpu.SemaphoreType.DMA((CHUNKS,)),
            pltpu.SemaphoreType.DMA((CHUNKS,)),
            pltpu.SemaphoreType.DMA((CHUNKS,)),
            pltpu.SemaphoreType.DMA((2,)),
            pltpu.SemaphoreType.DMA((2,)),
        ],
        compiler_params=pltpu.CompilerParams(
            collective_id=0, has_side_effects=True, vmem_limit_bytes=50 << 20
        ),
    )(*operands)


def solution(mesh):
    return jax.shard_map(
        on_device,
        mesh=mesh,
        in_specs=(P(None, "rg", "az"), P("rg"), P("rg", "az"), P("rg", "az")),
        out_specs=P(None, "rg", "az"),
        check_vma=False,
    )
```

```python
import math

import jax
import jax.numpy as jnp
import numpy as np
from jax import lax
from jax.experimental import pallas as pl
from jax.experimental.pallas import tpu as pltpu
from jax.sharding import PartitionSpec as P

MESH = pl.DeviceIdType.MESH
N_AZ = 64
N_RG = 4
ROWS = 512
COLS = 512
FULL = N_AZ * COLS
LANES = 128
FIRST = 256
SECOND = 128
CHUNKS = 4
CHUNK_ROWS = ROWS // CHUNKS
PAIR = CHUNK_ROWS // N_AZ
BLOCK = PAIR * 8
CHUNK_FLAT = N_AZ * BLOCK
FLAT = CHUNKS * CHUNK_FLAT
BEFORE = 8
AFTER = 72
FOCUS_ROWS = BEFORE + ROWS + AFTER + 8
TAPS = 15
EARLY = 7


def split(array):
    high = array.astype(jnp.bfloat16)
    low = (array - np.asarray(high).astype(np.float64)).astype(jnp.bfloat16)
    return high, low


def dft_tables():
    a = np.arange(FIRST)
    angle = 2.0 * np.pi * (np.outer(a, a) % FIRST) / FIRST
    cosine = np.cos(angle).reshape(FIRST, N_AZ, 4)
    sine = np.sin(angle).reshape(FIRST, N_AZ, 4)
    first = np.stack(
        [np.stack([cosine, sine], axis=2), np.stack([-sine, cosine], axis=2)], axis=0
    ).reshape(2 * FIRST, N_AZ * 8)
    angle = 2.0 * np.pi * (np.outer(a, np.arange(SECOND)) % FULL) / FULL
    norm = 1.0 / math.sqrt(FULL)
    twiddle = np.stack([np.cos(angle), np.sin(angle)]) * norm
    b = np.arange(SECOND)
    angle = 2.0 * np.pi * (np.outer(b, b) % SECOND) / SECOND
    cosine = np.cos(angle).reshape(N_AZ, 2, SECOND).transpose(1, 0, 2)
    sine = np.sin(angle).reshape(N_AZ, 2, SECOND).transpose(1, 0, 2)
    second = np.stack(
        [np.concatenate([cosine, sine], axis=2), np.concatenate([-sine, cosine], axis=2)], axis=0
    ).reshape(2 * SECOND, 2 * SECOND)
    first_high, first_low = split(first)
    second_high, second_low = split(second)
    return first_high, first_low, second_high, second_low, twiddle.astype(np.float32)


def sin_cos_of(rest, count):
    sign = 1.0 - 2.0 * (count - 2.0 * jnp.floor(count * 0.5))
    square = rest * rest
    sine = -1.0 / math.factorial(11)
    for order in (9, 7, 5, 3, 1):
        sine = sine * square + (-1.0) ** (order // 2) / math.factorial(order)
    cosine = 1.0 / math.factorial(12)
    for order in (10, 8, 6, 4, 2, 0):
        cosine = cosine * square + (-1.0) ** (order // 2) / math.factorial(order)
    return sine * rest * sign, cosine * sign


def sin_cos(angle):
    count = jnp.floor(angle * (1.0 / math.pi) + 0.5)
    rest = (angle - count * 3.140625) - count * (math.pi - 3.140625)
    return sin_cos_of(rest, count)


def sin_cos_pi(turns):
    count = jnp.floor(turns + 0.5)
    return sin_cos_of((turns - count) * math.pi, count)


def dot3(table_high, table_low, value, contract_on):
    high = value.astype(jnp.bfloat16)
    low = (value - high.astype(jnp.float32)).astype(jnp.bfloat16)
    dims = (((1,), (contract_on,)), ((), ()))
    dot = lambda left, right: lax.dot_general(left, right, dims, preferred_element_type=jnp.float32)
    return dot(table_high, high) + (dot(table_high, low) + dot(table_low, high))


def map_rows(out_ref, focus, weights, coarse, window, seg, first, count):
    def body(tile, carry):
        index = seg * 4 + tile
        h = coarse[index]
        eight = h >= 8
        four = (h & 4) != 0
        two = (h & 2) != 0
        one = (h & 1) != 0
        taps = [jnp.broadcast_to(weights[index, m : m + 1, :], (8, LANES)) for m in range(TAPS)]
        for part in range(2):
            plane = part * 4 + tile
            need = count + 3
            base = (seg * 16 + first) * 8 if isinstance(seg, int) else pl.multiple_of((seg * 16 + first) * 8, 8)
            load = lambda i: focus[plane, pl.ds(base + i * 8, 8), :]
            tiles = [load(i) for i in range(need + 8)]
            step = [
                jnp.where(eight, tiles[i + 8], tiles[i]) if i < need else tiles[i]
                for i in range(need + 7)
            ]
            step = [jnp.where(four, step[i + 4], step[i]) for i in range(need + 3)]
            step = [jnp.where(two, step[i + 2], step[i]) for i in range(need + 1)]
            for i in range(need):
                window[part, i * 8 : i * 8 + 8, :] = jnp.where(one, step[i + 1], step[i])
            for i in range(count):
                total = None
                for m in range(TAPS):
                    term = taps[m] * window[part, i * 8 + 5 + m : i * 8 + 13 + m, :]
                    total = term if total is None else total + term
                out_ref[part, pl.ds(base + i * 8, 8), pl.ds(pl.multiple_of(tile * LANES, LANES), LANES)] = total
        return carry

    lax.fori_loop(0, 4, body, 0)


def kernel(
    echo_hbm, chirp_hbm, shift_hbm, tap_hbm, t1h_hbm, t1l_hbm, t2h_hbm, t2l_hbm, tw_hbm,
    out_ref, focus, weights, coarse,
    echo, chirp_ref, shift_ref, tap_ref, t1h, t1l, t2h, t2l, tw, out_flat, in_flat, spec_flat, back_flat, phase_cos, phase_sin,
    chirp_cos, chirp_sin, window,
    load_sem, table_sem, send1, recv1, send2, recv2, halo_send, halo_recv,
):
    me = lax.axis_index("az")
    rg = lax.axis_index("rg")
    up = lax.rem(rg + 1, N_RG)
    down = lax.rem(rg + N_RG - 1, N_RG)

    barrier = pltpu.get_barrier_semaphore()

    def greet(i, carry):
        pl.semaphore_signal(
            barrier, inc=1, device_id=(lax.rem(me + i, N_AZ), rg), device_id_type=MESH
        )
        return carry

    chirp_copy = pltpu.make_async_copy(chirp_hbm, chirp_ref, table_sem.at[5])
    chirp_copy.start()
    echo_copies = []
    for chunk in range(CHUNKS):
        rows = pl.ds(chunk * CHUNK_ROWS, CHUNK_ROWS)
        echo_copies.append(
            pltpu.make_async_copy(echo_hbm.at[:, rows], echo.at[:, rows], load_sem.at[chunk])
        )
        echo_copies[-1].start()
    lax.fori_loop(1, N_AZ, greet, 0)
    for other in (up, down):
        pl.semaphore_signal(barrier, inc=1, device_id=(me, other), device_id_type=MESH)
    table_copies = []
    for index, (source, target) in enumerate(
        (
            (t1h_hbm, t1h), (t1l_hbm, t1l), (t2h_hbm, t2h), (t2l_hbm, t2l), (tw_hbm, tw),
        )
    ):
        table_copies.append(pltpu.make_async_copy(source, target, table_sem.at[index]))
        table_copies[-1].start()

    shift_copy = pltpu.make_async_copy(shift_hbm, shift_ref, table_sem.at[6])
    tap_copy = pltpu.make_async_copy(tap_hbm, tap_ref, table_sem.at[7])
    shift_copy.start()
    tap_copy.start()

    chirp_copy.wait()
    sine, cosine = sin_cos_pi(chirp_ref[...] * (1.0 / math.pi))
    for part in range(ROWS // LANES):
        rows = pl.ds(part * LANES, LANES)
        chirp_cos[rows, :] = jnp.transpose(
            jnp.broadcast_to(cosine[part : part + 1, :], (LANES, LANES))
        )
        chirp_sin[rows, :] = jnp.transpose(
            jnp.broadcast_to(sine[part : part + 1, :], (LANES, LANES))
        )

    def matched(chunk):
        def body(i, carry):
            row = pl.multiple_of(chunk * CHUNK_ROWS + i * 8, 8)
            c = chirp_cos[pl.ds(row, 8), :]
            s = chirp_sin[pl.ds(row, 8), :]
            for tile in range(4):
                lanes = slice(tile * LANES, (tile + 1) * LANES)
                re = echo[0, pl.ds(row, 8), lanes]
                im = echo[1, pl.ds(row, 8), lanes]
                out_flat[pl.ds(row * 8 + tile, 8, stride=8), :] = re * c + im * s
                out_flat[pl.ds(row * 8 + 4 + tile, 8, stride=8), :] = im * c - re * s
            return carry

        lax.fori_loop(0, CHUNK_ROWS // 8, body, 0)

    def exchange(source, target, send, recv, chunk, beside=None):
        def body(i, carry):
            other = lax.rem(me + i, N_AZ)
            away = pl.multiple_of(chunk * CHUNK_FLAT + other * BLOCK, BLOCK)
            home = pl.multiple_of(chunk * CHUNK_FLAT + me * BLOCK, BLOCK)
            pltpu.make_async_remote_copy(
                src_ref=source.at[pl.ds(away, BLOCK)],
                dst_ref=target.at[pl.ds(home, BLOCK)],
                send_sem=send.at[chunk],
                recv_sem=recv.at[chunk],
                device_id=(other, rg),
                device_id_type=MESH,
            ).start()
            if beside is not None:
                beside(i - 1)
            return carry

        lax.fori_loop(1, N_AZ, body, 0)
        home = pl.multiple_of(chunk * CHUNK_FLAT + me * BLOCK, BLOCK)
        target[pl.ds(home, BLOCK), :] = source[pl.ds(home, BLOCK), :]

    def all_of(source, target, send, recv, chunk):
        rows = pl.ds(pl.multiple_of(chunk * CHUNK_FLAT, BLOCK), CHUNK_FLAT - BLOCK)
        return pltpu.make_async_remote_copy(
            src_ref=source.at[rows],
            dst_ref=target.at[rows],
            send_sem=send.at[chunk],
            recv_sem=recv.at[chunk],
            device_id=(lax.rem(me + 1, N_AZ), rg),
            device_id_type=MESH,
        )

    echo_copies[0].wait()
    matched(0)
    pl.semaphore_wait(barrier, N_AZ + 1)
    exchange(out_flat, in_flat, send1, recv1, 0)
    echo_copies[3].wait()
    matched(3)
    exchange(out_flat, in_flat, send1, recv1, 3)
    for chunk in (2, 1):
        echo_copies[chunk].wait()
        matched(chunk)

    lane_id = lax.broadcasted_iota(jnp.int32, (8, LANES), 1)
    row_id = lax.broadcasted_iota(jnp.int32, (8, LANES), 0)

    def phase_body(i, carry):
        row = pl.multiple_of(i * 8, 8)
        r = 1.0 + (rg * ROWS + row + row_id).astype(jnp.float32) * (1.0 / (ROWS * N_RG))
        rr = r * r
        for tile in range(4):
            line = me * COLS + tile * LANES + lane_id
            signed = jnp.where(line < FULL // 2, line, line - FULL)
            q = signed.astype(jnp.float32) * (0.9 / (FULL // 2))
            s, c = sin_cos(40.0 * jnp.sqrt(rr - q * q))
            phase_cos[tile, pl.ds(row, 8), :] = c
            phase_sin[tile, pl.ds(row, 8), :] = s
        return carry

    lax.fori_loop(0, ROWS // 8, phase_body, 0)

    shift_copy.wait()
    tap_copy.wait()
    tap_id = lax.broadcasted_iota(jnp.int32, (16, LANES), 0)
    for seg in range(CHUNKS):
        for tile in range(4):
            lanes = slice(tile * LANES, (tile + 1) * LANES)
            shift = shift_ref[seg : seg + 1, lanes]
            slot = tap_id - jnp.broadcast_to(shift & 7, (16, LANES))
            frac = jnp.broadcast_to(tap_ref[seg : seg + 1, lanes], (16, LANES))
            u = (slot - 3).astype(jnp.float32) - frac.astype(jnp.float32) * (1.0 / 16.0)
            sine, _ = sin_cos_pi(u)
            _, cosine = sin_cos_pi(u * 0.25)
            at_zero = u == 0.0
            sinc = jnp.where(at_zero, 1.0, sine / jnp.where(at_zero, 1.0, u * math.pi))
            inside = jnp.logical_and(slot >= 0, slot < 8)
            weights[seg * 4 + tile] = jnp.where(inside, sinc * (0.54 + 0.46 * cosine), 0.0)
            coarse[seg * 4 + tile] = jnp.broadcast_to(shift >> 3, (8, LANES))

    for plane in range(8):
        focus[plane, pl.ds(BEFORE, ROWS), :] = jnp.zeros((ROWS, LANES), jnp.float32)
        focus[plane, pl.ds(BEFORE + ROWS + AFTER, 8), :] = jnp.zeros((8, LANES), jnp.float32)

    for copy in table_copies:
        copy.wait()

    def transform(chunk):
        all_of(out_flat, in_flat, send1, recv1, chunk).wait_recv()
        start = pl.multiple_of(chunk * CHUNK_FLAT, CHUNK_FLAT)
        both = in_flat[pl.ds(start, CHUNK_FLAT), :].reshape(N_AZ, PAIR, 8, LANES)
        signal = jnp.concatenate(
            [both[:, pair].reshape(N_AZ * 8, LANES) for pair in range(PAIR)], axis=1
        )
        section = dot3(t1h[...], t1l[...], signal, 0)
        for pair in range(PAIR):
            lanes = slice(pair * LANES, (pair + 1) * LANES)
            re = section[:FIRST, lanes]
            im = section[FIRST:, lanes]
            turned = jnp.concatenate([re * tw[0] + im * tw[1], im * tw[0] - re * tw[1]], axis=1)
            final = dot3(t2h[...], t2l[...], turned, 1)
            for quarter in range(4):
                for half in range(2):
                    spec_flat[pl.ds(start + pair * 8 + quarter * 2 + half, N_AZ, stride=BLOCK), :] = (
                        final[quarter * N_AZ : (quarter + 1) * N_AZ, half * LANES : (half + 1) * LANES]
                    )
        exchange(spec_flat, back_flat, send2, recv2, chunk)

    def focus_rows(chunk):
        all_of(spec_flat, back_flat, send2, recv2, chunk).wait_recv()

        def body(i, carry):
            row = pl.multiple_of(chunk * CHUNK_ROWS + i * 8, 8)
            for tile in range(4):
                a = back_flat[pl.ds(row * 8 + tile, 8, stride=8), :]
                b = back_flat[pl.ds(row * 8 + 4 + tile, 8, stride=8), :]
                c = phase_cos[tile, pl.ds(row, 8), :]
                s = phase_sin[tile, pl.ds(row, 8), :]
                focus[tile, pl.ds(BEFORE + row, 8), :] = a * c - b * s
                focus[4 + tile, pl.ds(BEFORE + row, 8), :] = a * s + b * c
            return carry

        lax.fori_loop(0, CHUNK_ROWS // 8, body, 0)

    def stolt(seg, first, count):
        map_rows(out_ref, focus, weights, coarse, window, seg, first, count)

    def halo(towards, source_row, target_row, which):
        def piece(plane, start, count):
            return pltpu.make_async_remote_copy(
                src_ref=focus.at[plane, pl.ds(source_row + start, count)],
                dst_ref=focus.at[plane, pl.ds(target_row + start, count)],
                send_sem=halo_send.at[which],
                recv_sem=halo_recv.at[which],
                device_id=(me, towards),
                device_id_type=MESH,
            )

        return piece

    down_piece = halo(down, BEFORE, BEFORE + ROWS, 0)
    up_piece = halo(up, BEFORE + ROWS - BEFORE, 0, 1)
    to_down = down_piece(slice(None), 0, AFTER)
    to_up = up_piece(slice(None), 0, BEFORE)

    def send_down(piece):
        down_piece(piece // 9, pl.multiple_of(piece % 9 * 8, 8), 8).start()

    def step(k, carry):
        now = (CHUNKS - k) % CHUNKS
        transform(now)

        @pl.when(k == 0)
        def _():
            exchange(out_flat, in_flat, send1, recv1, 2)

        @pl.when(k >= 1)
        def _():
            focus_rows((CHUNKS + 1 - k) % CHUNKS)

        @pl.when(k == 1)
        def _():
            exchange(out_flat, in_flat, send1, recv1, 1, beside=send_down)
            for piece in range(N_AZ - 1, 72):
                send_down(piece)

        @pl.when(k == 2)
        def _():
            for plane in range(8):
                up_piece(plane, 0, BEFORE).start()
            to_down.wait_recv()

            @pl.when(rg == N_RG - 1)
            def _():
                focus[:, pl.ds(BEFORE + ROWS, AFTER), :] = jnp.zeros((8, AFTER, LANES), jnp.float32)

        @pl.when(k >= 2)
        def _():
            seg = CHUNKS + 1 - k
            stolt(seg, 1, EARLY - 1)
            stolt(seg, EARLY, 16 - EARLY)

        return carry

    lax.fori_loop(0, CHUNKS, step, 0)
    stolt(3, 0, 1)
    to_up.wait_recv()

    @pl.when(rg == 0)
    def _():
        focus[:, pl.ds(0, BEFORE), :] = jnp.zeros((8, BEFORE, LANES), jnp.float32)

    stolt(0, 0, EARLY)
    focus_rows(1)
    to_down.wait_send()
    to_up.wait_send()
    for chunk in range(CHUNKS):
        all_of(out_flat, in_flat, send1, recv1, chunk).wait_send()
        all_of(spec_flat, back_flat, send2, recv2, chunk).wait_send()


LATE = ((0, EARLY, 16 - EARLY), (1, 0, EARLY), (1, EARLY, 16 - EARLY), (2, 0, 1))


def finish(part_ref, focus, weights, coarse, out_hbm, late, window, store_sem):
    copies = []

    def store(source, first, end):
        rows = pl.ds(first, end - first)
        copies.append(
            pltpu.make_async_copy(
                source.at[:, rows], out_hbm.at[:, rows], store_sem.at[len(copies)]
            )
        )
        copies[-1].start()

    store(part_ref, 0, EARLY * 8)
    store(part_ref, (2 * 16 + 1) * 8, ROWS)
    for seg, first, count in LATE:
        map_rows(late, focus, weights, coarse, window, seg, first, count)
        store(late, (seg * 16 + first) * 8, (seg * 16 + first + count) * 8)
    for copy in copies:
        copy.wait()


def on_device(echo_data, chirp_phase, stolt_shift, tap_index):
    tables = [jnp.asarray(table) for table in dft_tables()]
    vmem_spec = pl.BlockSpec(memory_space=pltpu.VMEM)
    hbm_spec = pl.BlockSpec(memory_space=pltpu.HBM)
    f32 = jnp.float32
    chirp = chirp_phase.reshape(ROWS // LANES, LANES)
    operands = [
        pltpu.with_memory_space_constraint(operand, pltpu.HBM)
        for operand in (echo_data, chirp, stolt_shift, tap_index, *tables)
    ]
    first = pl.pallas_call(
        kernel,
        out_shape=[
            pltpu.VMEM((2, ROWS, COLS), f32),
            pltpu.VMEM((8, FOCUS_ROWS, LANES), f32),
            pltpu.VMEM((16, 16, LANES), f32),
            pltpu.VMEM((16, 8, LANES), jnp.int32),
        ],
        in_specs=[hbm_spec] * 9,
        out_specs=[vmem_spec] * 4,
        scratch_shapes=[
            pltpu.VMEM((2, ROWS, COLS), f32),
            pltpu.VMEM((ROWS // LANES, LANES), f32),
            pltpu.VMEM((CHUNKS, COLS), jnp.int32),
            pltpu.VMEM((CHUNKS, COLS), jnp.int32),
            pltpu.VMEM((512, 512), jnp.bfloat16),
            pltpu.VMEM((512, 512), jnp.bfloat16),
            pltpu.VMEM((256, 256), jnp.bfloat16),
            pltpu.VMEM((256, 256), jnp.bfloat16),
            pltpu.VMEM((2, FIRST, SECOND), f32),
            pltpu.VMEM((FLAT, LANES), f32),
            pltpu.VMEM((FLAT, LANES), f32),
            pltpu.VMEM((FLAT, LANES), f32),
            pltpu.VMEM((FLAT, LANES), f32),
            pltpu.VMEM((4, ROWS, LANES), f32),
            pltpu.VMEM((4, ROWS, LANES), f32),
            pltpu.VMEM((ROWS, LANES), f32),
            pltpu.VMEM((ROWS, LANES), f32),
            pltpu.VMEM((2, 160, LANES), f32),
            pltpu.SemaphoreType.DMA((CHUNKS,)),
            pltpu.SemaphoreType.DMA((8,)),
            pltpu.SemaphoreType.DMA((CHUNKS,)),
            pltpu.SemaphoreType.DMA((CHUNKS,)),
            pltpu.SemaphoreType.DMA((CHUNKS,)),
            pltpu.SemaphoreType.DMA((CHUNKS,)),
            pltpu.SemaphoreType.DMA((2,)),
            pltpu.SemaphoreType.DMA((2,)),
        ],
        compiler_params=pltpu.CompilerParams(
            collective_id=0, has_side_effects=True, vmem_limit_bytes=50 << 20
        ),
    )(*operands)
    return pl.pallas_call(
        finish,
        out_shape=jax.ShapeDtypeStruct((2, ROWS, COLS), f32),
        in_specs=[vmem_spec] * 4,
        out_specs=hbm_spec,
        scratch_shapes=[
            pltpu.VMEM((2, ROWS, COLS), f32),
            pltpu.VMEM((2, 160, LANES), f32),
            pltpu.SemaphoreType.DMA((2 + len(LATE),)),
        ],
        compiler_params=pltpu.CompilerParams(vmem_limit_bytes=16 << 20),
    )(*first)


def solution(mesh):
    return jax.shard_map(
        on_device,
        mesh=mesh,
        in_specs=(P(None, "rg", "az"), P("rg"), P("rg", "az"), P("rg", "az")),
        out_specs=P(None, "rg", "az"),
        check_vma=False,
    )
```

```python
import math

import jax
import jax.numpy as jnp
import numpy as np
from jax import lax
from jax.experimental import pallas as pl
from jax.experimental.pallas import tpu as pltpu
from jax.sharding import PartitionSpec as P

MESH = pl.DeviceIdType.MESH
N_AZ = 64
N_RG = 4
ROWS = 512
COLS = 512
FULL = N_AZ * COLS
LANES = 128
FIRST = 256
SECOND = 128
CHUNKS = 4
CHUNK_ROWS = ROWS // CHUNKS
PAIR = CHUNK_ROWS // N_AZ
BLOCK = PAIR * 8
CHUNK_FLAT = N_AZ * BLOCK
FLAT = CHUNKS * CHUNK_FLAT
BEFORE = 8
AFTER = 72
FOCUS_ROWS = BEFORE + ROWS + AFTER + 8
TAPS = 15
EARLY = 7
LAST = 1
HALF_TILES = 8


def split(array):
    high = array.astype(jnp.bfloat16)
    low = (array - np.asarray(high).astype(np.float64)).astype(jnp.bfloat16)
    return high, low


def dft_tables():
    a = np.arange(FIRST)
    angle = 2.0 * np.pi * (np.outer(a, a) % FIRST) / FIRST
    cosine = np.cos(angle).reshape(FIRST, N_AZ, 4)
    sine = np.sin(angle).reshape(FIRST, N_AZ, 4)
    first = np.stack(
        [np.stack([cosine, sine], axis=2), np.stack([-sine, cosine], axis=2)], axis=0
    ).reshape(2 * FIRST, N_AZ * 8)
    angle = 2.0 * np.pi * (np.outer(a, np.arange(SECOND)) % FULL) / FULL
    norm = 1.0 / math.sqrt(FULL)
    twiddle = np.stack([np.cos(angle), np.sin(angle)]) * norm
    b = np.arange(SECOND)
    angle = 2.0 * np.pi * (np.outer(b, b) % SECOND) / SECOND
    cosine = np.cos(angle).reshape(N_AZ, 2, SECOND).transpose(1, 0, 2)
    sine = np.sin(angle).reshape(N_AZ, 2, SECOND).transpose(1, 0, 2)
    second = np.stack(
        [np.concatenate([cosine, sine], axis=2), np.concatenate([-sine, cosine], axis=2)], axis=0
    ).reshape(2 * SECOND, 2 * SECOND)
    first_high, first_low = split(first)
    second_high, second_low = split(second)
    return first_high, first_low, second_high, second_low, twiddle.astype(np.float32)


def sin_cos_of(rest, count):
    sign = 1.0 - 2.0 * (count - 2.0 * jnp.floor(count * 0.5))
    square = rest * rest
    sine = -1.0 / math.factorial(11)
    for order in (9, 7, 5, 3, 1):
        sine = sine * square + (-1.0) ** (order // 2) / math.factorial(order)
    cosine = 1.0 / math.factorial(12)
    for order in (10, 8, 6, 4, 2, 0):
        cosine = cosine * square + (-1.0) ** (order // 2) / math.factorial(order)
    return sine * rest * sign, cosine * sign


def sin_cos(angle):
    count = jnp.floor(angle * (1.0 / math.pi) + 0.5)
    rest = (angle - count * 3.140625) - count * (math.pi - 3.140625)
    return sin_cos_of(rest, count)


def sin_cos_pi(turns):
    count = jnp.floor(turns + 0.5)
    return sin_cos_of((turns - count) * math.pi, count)


def dot3(table_high, table_low, value, contract_on):
    high = value.astype(jnp.bfloat16)
    low = (value - high.astype(jnp.float32)).astype(jnp.bfloat16)
    dims = (((1,), (contract_on,)), ((), ()))
    dot = lambda left, right: lax.dot_general(left, right, dims, preferred_element_type=jnp.float32)
    return dot(table_high, high) + (dot(table_high, low) + dot(table_low, high))


def map_rows(out_ref, focus, weights, coarse, window, seg, first, count):
    def body(tile, carry):
        index = seg * 4 + tile
        h = coarse[index]
        eight = h >= 8
        four = (h & 4) != 0
        two = (h & 2) != 0
        one = (h & 1) != 0
        taps = [jnp.broadcast_to(weights[index, m : m + 1, :], (8, LANES)) for m in range(TAPS)]
        for part in range(2):
            plane = part * 4 + tile
            need = count + 3
            base = (seg * 16 + first) * 8 if isinstance(seg, int) else pl.multiple_of((seg * 16 + first) * 8, 8)
            load = lambda i: focus[plane, pl.ds(base + i * 8, 8), :]
            tiles = [load(i) for i in range(need + 8)]
            step = [
                jnp.where(eight, tiles[i + 8], tiles[i]) if i < need else tiles[i]
                for i in range(need + 7)
            ]
            step = [jnp.where(four, step[i + 4], step[i]) for i in range(need + 3)]
            step = [jnp.where(two, step[i + 2], step[i]) for i in range(need + 1)]
            for i in range(need):
                window[part, i * 8 : i * 8 + 8, :] = jnp.where(one, step[i + 1], step[i])
            for i in range(count):
                total = None
                for m in range(TAPS):
                    term = taps[m] * window[part, i * 8 + 5 + m : i * 8 + 13 + m, :]
                    total = term if total is None else total + term
                out_ref[part, pl.ds(base + i * 8, 8), pl.ds(pl.multiple_of(tile * LANES, LANES), LANES)] = total
        return carry

    lax.fori_loop(0, 4, body, 0)


def kernel(
    echo_hbm, chirp_hbm, shift_hbm, tap_hbm, t1h_hbm, t1l_hbm, t2h_hbm, t2l_hbm, tw_hbm,
    out_ref, focus, weights, coarse,
    echo, chirp_ref, shift_ref, tap_ref, t1h, t1l, t2h, t2l, tw, out_flat, in_flat, spec_flat, back_flat, phase_cos, phase_sin,
    chirp_cos, chirp_sin, window,
    load_sem, table_sem, send1, recv1, send2, recv2, halo_send, halo_recv, half_send, half_recv,
):
    me = lax.axis_index("az")
    rg = lax.axis_index("rg")
    up = lax.rem(rg + 1, N_RG)
    down = lax.rem(rg + N_RG - 1, N_RG)

    barrier = pltpu.get_barrier_semaphore()

    def greet(i, carry):
        pl.semaphore_signal(
            barrier, inc=1, device_id=(lax.rem(me + i, N_AZ), rg), device_id_type=MESH
        )
        return carry

    chirp_copy = pltpu.make_async_copy(chirp_hbm, chirp_ref, table_sem.at[5])
    chirp_copy.start()
    echo_copies = []
    for chunk in range(CHUNKS):
        rows = pl.ds(chunk * CHUNK_ROWS, CHUNK_ROWS)
        echo_copies.append(
            pltpu.make_async_copy(echo_hbm.at[:, rows], echo.at[:, rows], load_sem.at[chunk])
        )
        echo_copies[-1].start()
    lax.fori_loop(1, N_AZ, greet, 0)
    for other in (up, down):
        pl.semaphore_signal(barrier, inc=1, device_id=(me, other), device_id_type=MESH)
    table_copies = []
    for index, (source, target) in enumerate(
        (
            (t1h_hbm, t1h), (t1l_hbm, t1l), (t2h_hbm, t2h), (t2l_hbm, t2l), (tw_hbm, tw),
        )
    ):
        table_copies.append(pltpu.make_async_copy(source, target, table_sem.at[index]))
        table_copies[-1].start()

    shift_copy = pltpu.make_async_copy(shift_hbm, shift_ref, table_sem.at[6])
    tap_copy = pltpu.make_async_copy(tap_hbm, tap_ref, table_sem.at[7])
    shift_copy.start()
    tap_copy.start()

    chirp_copy.wait()
    sine, cosine = sin_cos_pi(chirp_ref[...] * (1.0 / math.pi))
    for part in range(ROWS // LANES):
        rows = pl.ds(part * LANES, LANES)
        chirp_cos[rows, :] = jnp.transpose(
            jnp.broadcast_to(cosine[part : part + 1, :], (LANES, LANES))
        )
        chirp_sin[rows, :] = jnp.transpose(
            jnp.broadcast_to(sine[part : part + 1, :], (LANES, LANES))
        )

    def matched(chunk):
        def body(i, carry):
            row = pl.multiple_of(chunk * CHUNK_ROWS + i * 8, 8)
            c = chirp_cos[pl.ds(row, 8), :]
            s = chirp_sin[pl.ds(row, 8), :]
            for tile in range(4):
                lanes = slice(tile * LANES, (tile + 1) * LANES)
                re = echo[0, pl.ds(row, 8), lanes]
                im = echo[1, pl.ds(row, 8), lanes]
                out_flat[pl.ds(row * 8 + tile, 8, stride=8), :] = re * c + im * s
                out_flat[pl.ds(row * 8 + 4 + tile, 8, stride=8), :] = im * c - re * s
            return carry

        lax.fori_loop(0, CHUNK_ROWS // 8, body, 0)

    def exchange(source, target, send, recv, chunk, beside=None):
        def body(i, carry):
            other = lax.rem(me + i, N_AZ)
            away = pl.multiple_of(chunk * CHUNK_FLAT + other * BLOCK, BLOCK)
            home = pl.multiple_of(chunk * CHUNK_FLAT + me * BLOCK, BLOCK)
            pltpu.make_async_remote_copy(
                src_ref=source.at[pl.ds(away, BLOCK)],
                dst_ref=target.at[pl.ds(home, BLOCK)],
                send_sem=send.at[chunk],
                recv_sem=recv.at[chunk],
                device_id=(other, rg),
                device_id_type=MESH,
            ).start()
            if beside is not None:
                beside(i - 1)
            return carry

        lax.fori_loop(1, N_AZ, body, 0)
        home = pl.multiple_of(chunk * CHUNK_FLAT + me * BLOCK, BLOCK)
        target[pl.ds(home, BLOCK), :] = source[pl.ds(home, BLOCK), :]

    def half_row(half, device):
        return pl.multiple_of(LAST * CHUNK_FLAT + half * CHUNK_FLAT // 2 + device * 8, 8)

    def own_row(half, device):
        return pl.multiple_of(LAST * CHUNK_FLAT + device * BLOCK + half * 8, 8)

    def exchange_half(source, source_row, target, target_row, send, recv, half, beside=None):
        def body(i, carry):
            other = lax.rem(me + i, N_AZ)
            pltpu.make_async_remote_copy(
                src_ref=source.at[pl.ds(source_row(half, other), 8)],
                dst_ref=target.at[pl.ds(target_row(half, me), 8)],
                send_sem=send,
                recv_sem=recv,
                device_id=(other, rg),
                device_id_type=MESH,
            ).start()
            if beside is not None:
                beside(i - 1)
            return carry

        lax.fori_loop(1, N_AZ, body, 0)
        target[pl.ds(target_row(half, me), 8), :] = source[pl.ds(source_row(half, me), 8), :]

    def half_of(half):
        rows = pl.ds(LAST * CHUNK_FLAT + half * CHUNK_FLAT // 2, CHUNK_FLAT // 2 - 8)
        return pltpu.make_async_remote_copy(
            src_ref=spec_flat.at[rows],
            dst_ref=back_flat.at[rows],
            send_sem=half_send.at[half],
            recv_sem=half_recv.at[half],
            device_id=(lax.rem(me + 1, N_AZ), rg),
            device_id_type=MESH,
        )

    def all_of(source, target, send, recv, chunk):
        rows = pl.ds(pl.multiple_of(chunk * CHUNK_FLAT, BLOCK), CHUNK_FLAT - BLOCK)
        return pltpu.make_async_remote_copy(
            src_ref=source.at[rows],
            dst_ref=target.at[rows],
            send_sem=send.at[chunk],
            recv_sem=recv.at[chunk],
            device_id=(lax.rem(me + 1, N_AZ), rg),
            device_id_type=MESH,
        )

    echo_copies[0].wait()
    matched(0)
    pl.semaphore_wait(barrier, N_AZ + 1)
    exchange(out_flat, in_flat, send1, recv1, 0)
    echo_copies[3].wait()
    matched(3)
    exchange(out_flat, in_flat, send1, recv1, 3)
    for chunk in (2, 1):
        echo_copies[chunk].wait()
        matched(chunk)

    lane_id = lax.broadcasted_iota(jnp.int32, (8, LANES), 1)
    row_id = lax.broadcasted_iota(jnp.int32, (8, LANES), 0)

    def phase_body(i, carry):
        row = pl.multiple_of(i * 8, 8)
        r = 1.0 + (rg * ROWS + row + row_id).astype(jnp.float32) * (1.0 / (ROWS * N_RG))
        rr = r * r
        for tile in range(4):
            line = me * COLS + tile * LANES + lane_id
            signed = jnp.where(line < FULL // 2, line, line - FULL)
            q = signed.astype(jnp.float32) * (0.9 / (FULL // 2))
            s, c = sin_cos(40.0 * jnp.sqrt(rr - q * q))
            phase_cos[tile, pl.ds(row, 8), :] = c
            phase_sin[tile, pl.ds(row, 8), :] = s
        return carry

    lax.fori_loop(0, ROWS // 8, phase_body, 0)

    shift_copy.wait()
    tap_copy.wait()
    tap_id = lax.broadcasted_iota(jnp.int32, (16, LANES), 0)
    for seg in range(CHUNKS):
        for tile in range(4):
            lanes = slice(tile * LANES, (tile + 1) * LANES)
            shift = shift_ref[seg : seg + 1, lanes]
            slot = tap_id - jnp.broadcast_to(shift & 7, (16, LANES))
            frac = jnp.broadcast_to(tap_ref[seg : seg + 1, lanes], (16, LANES))
            u = (slot - 3).astype(jnp.float32) - frac.astype(jnp.float32) * (1.0 / 16.0)
            sine, _ = sin_cos_pi(u)
            _, cosine = sin_cos_pi(u * 0.25)
            at_zero = u == 0.0
            sinc = jnp.where(at_zero, 1.0, sine / jnp.where(at_zero, 1.0, u * math.pi))
            inside = jnp.logical_and(slot >= 0, slot < 8)
            weights[seg * 4 + tile] = jnp.where(inside, sinc * (0.54 + 0.46 * cosine), 0.0)
            coarse[seg * 4 + tile] = jnp.broadcast_to(shift >> 3, (8, LANES))

    for plane in range(8):
        focus[plane, pl.ds(BEFORE, ROWS), :] = jnp.zeros((ROWS, LANES), jnp.float32)
        focus[plane, pl.ds(BEFORE + ROWS + AFTER, 8), :] = jnp.zeros((8, LANES), jnp.float32)

    for copy in table_copies:
        copy.wait()

    def transform(chunk):
        all_of(out_flat, in_flat, send1, recv1, chunk).wait_recv()
        start = pl.multiple_of(chunk * CHUNK_FLAT, CHUNK_FLAT)
        both = in_flat[pl.ds(start, CHUNK_FLAT), :].reshape(N_AZ, PAIR, 8, LANES)
        signal = jnp.concatenate(
            [both[:, pair].reshape(N_AZ * 8, LANES) for pair in range(PAIR)], axis=1
        )
        section = dot3(t1h[...], t1l[...], signal, 0)
        for pair in range(PAIR):
            lanes = slice(pair * LANES, (pair + 1) * LANES)
            re = section[:FIRST, lanes]
            im = section[FIRST:, lanes]
            turned = jnp.concatenate([re * tw[0] + im * tw[1], im * tw[0] - re * tw[1]], axis=1)
            final = dot3(t2h[...], t2l[...], turned, 1)
            for quarter in range(4):
                for half in range(2):
                    spec_flat[pl.ds(start + pair * 8 + quarter * 2 + half, N_AZ, stride=BLOCK), :] = (
                        final[quarter * N_AZ : (quarter + 1) * N_AZ, half * LANES : (half + 1) * LANES]
                    )

        @pl.when(chunk != LAST)
        def _():
            exchange(spec_flat, back_flat, send2, recv2, chunk)

        @pl.when(chunk == LAST)
        def _():
            for half in (1, 0):
                exchange_half(
                    spec_flat, own_row, back_flat, half_row,
                    half_send.at[half], half_recv.at[half], half,
                )

    def focus_rows(chunk):
        all_of(spec_flat, back_flat, send2, recv2, chunk).wait_recv()
        focus_tiles(chunk * 16, 16)

    def focus_half(half):
        half_of(half).wait_recv()
        focus_tiles(LAST * 16 + half * HALF_TILES, HALF_TILES)

    def focus_tiles(first, count):
        def body(i, carry):
            row = pl.multiple_of((first + i) * 8, 8)
            for tile in range(4):
                a = back_flat[pl.ds(row * 8 + tile, 8, stride=8), :]
                b = back_flat[pl.ds(row * 8 + 4 + tile, 8, stride=8), :]
                c = phase_cos[tile, pl.ds(row, 8), :]
                s = phase_sin[tile, pl.ds(row, 8), :]
                focus[tile, pl.ds(BEFORE + row, 8), :] = a * c - b * s
                focus[4 + tile, pl.ds(BEFORE + row, 8), :] = a * s + b * c
            return carry

        lax.fori_loop(0, count, body, 0)

    def stolt(seg, first, count):
        map_rows(out_ref, focus, weights, coarse, window, seg, first, count)

    def halo(towards, source_row, target_row, which):
        def piece(plane, start, count):
            return pltpu.make_async_remote_copy(
                src_ref=focus.at[plane, pl.ds(source_row + start, count)],
                dst_ref=focus.at[plane, pl.ds(target_row + start, count)],
                send_sem=halo_send.at[which],
                recv_sem=halo_recv.at[which],
                device_id=(me, towards),
                device_id_type=MESH,
            )

        return piece

    down_piece = halo(down, BEFORE, BEFORE + ROWS, 0)
    up_piece = halo(up, BEFORE + ROWS - BEFORE, 0, 1)
    to_down = down_piece(slice(None), 0, AFTER)
    to_up = up_piece(slice(None), 0, BEFORE)

    def send_down(piece):
        down_piece(piece // 9, pl.multiple_of(piece % 9 * 8, 8), 8).start()

    def step(k, carry):
        now = (CHUNKS - k) % CHUNKS
        transform(now)

        @pl.when(k == 0)
        def _():
            exchange(out_flat, in_flat, send1, recv1, 2)

        @pl.when(k >= 1)
        def _():
            focus_rows((CHUNKS + 1 - k) % CHUNKS)

        @pl.when(k == 1)
        def _():
            first = out_flat, half_row, in_flat, own_row, send1.at[LAST], recv1.at[LAST]
            exchange_half(*first, 0, beside=send_down)
            exchange_half(*first, 1)
            for piece in range(N_AZ - 1, 72):
                send_down(piece)

        @pl.when(k == 2)
        def _():
            for plane in range(8):
                up_piece(plane, 0, BEFORE).start()
            to_down.wait_recv()

            @pl.when(rg == N_RG - 1)
            def _():
                focus[:, pl.ds(BEFORE + ROWS, AFTER), :] = jnp.zeros((8, AFTER, LANES), jnp.float32)

        @pl.when(k >= 2)
        def _():
            seg = CHUNKS + 1 - k
            stolt(seg, 1, EARLY - 1)
            stolt(seg, EARLY, 16 - EARLY)

        return carry

    lax.fori_loop(0, CHUNKS, step, 0)
    stolt(3, 0, 1)
    to_up.wait_recv()

    @pl.when(rg == 0)
    def _():
        focus[:, pl.ds(0, BEFORE), :] = jnp.zeros((8, BEFORE, LANES), jnp.float32)

    stolt(0, 0, EARLY)
    focus_half(1)
    stolt(LAST, HALF_TILES + 1, 7)
    stolt(2, 0, 1)
    focus_half(0)
    to_down.wait_send()
    to_up.wait_send()
    for chunk in range(CHUNKS):
        all_of(out_flat, in_flat, send1, recv1, chunk).wait_send()
        if chunk != LAST:
            all_of(spec_flat, back_flat, send2, recv2, chunk).wait_send()
    for half in range(2):
        half_of(half).wait_send()


LATE = ((0, EARLY, 16 - EARLY), (LAST, 0, HALF_TILES + 1))


def finish(part_ref, focus, weights, coarse, out_hbm, late, window, store_sem):
    copies = []

    def store(source, first, end):
        rows = pl.ds(first, end - first)
        copies.append(
            pltpu.make_async_copy(
                source.at[:, rows], out_hbm.at[:, rows], store_sem.at[len(copies)]
            )
        )
        copies[-1].start()

    store(part_ref, 0, EARLY * 8)
    store(part_ref, (LAST * 16 + HALF_TILES + 1) * 8, ROWS)
    for seg, first, count in LATE:
        map_rows(late, focus, weights, coarse, window, seg, first, count)
        store(late, (seg * 16 + first) * 8, (seg * 16 + first + count) * 8)
    for copy in copies:
        copy.wait()


def on_device(echo_data, chirp_phase, stolt_shift, tap_index):
    tables = [jnp.asarray(table) for table in dft_tables()]
    vmem_spec = pl.BlockSpec(memory_space=pltpu.VMEM)
    hbm_spec = pl.BlockSpec(memory_space=pltpu.HBM)
    f32 = jnp.float32
    chirp = chirp_phase.reshape(ROWS // LANES, LANES)
    operands = [
        pltpu.with_memory_space_constraint(operand, pltpu.HBM)
        for operand in (echo_data, chirp, stolt_shift, tap_index, *tables)
    ]
    first = pl.pallas_call(
        kernel,
        out_shape=[
            pltpu.VMEM((2, ROWS, COLS), f32),
            pltpu.VMEM((8, FOCUS_ROWS, LANES), f32),
            pltpu.VMEM((16, 16, LANES), f32),
            pltpu.VMEM((16, 8, LANES), jnp.int32),
        ],
        in_specs=[hbm_spec] * 9,
        out_specs=[vmem_spec] * 4,
        scratch_shapes=[
            pltpu.VMEM((2, ROWS, COLS), f32),
            pltpu.VMEM((ROWS // LANES, LANES), f32),
            pltpu.VMEM((CHUNKS, COLS), jnp.int32),
            pltpu.VMEM((CHUNKS, COLS), jnp.int32),
            pltpu.VMEM((512, 512), jnp.bfloat16),
            pltpu.VMEM((512, 512), jnp.bfloat16),
            pltpu.VMEM((256, 256), jnp.bfloat16),
            pltpu.VMEM((256, 256), jnp.bfloat16),
            pltpu.VMEM((2, FIRST, SECOND), f32),
            pltpu.VMEM((FLAT, LANES), f32),
            pltpu.VMEM((FLAT, LANES), f32),
            pltpu.VMEM((FLAT, LANES), f32),
            pltpu.VMEM((FLAT, LANES), f32),
            pltpu.VMEM((4, ROWS, LANES), f32),
            pltpu.VMEM((4, ROWS, LANES), f32),
            pltpu.VMEM((ROWS, LANES), f32),
            pltpu.VMEM((ROWS, LANES), f32),
            pltpu.VMEM((2, 160, LANES), f32),
            pltpu.SemaphoreType.DMA((CHUNKS,)),
            pltpu.SemaphoreType.DMA((8,)),
            pltpu.SemaphoreType.DMA((CHUNKS,)),
            pltpu.SemaphoreType.DMA((CHUNKS,)),
            pltpu.SemaphoreType.DMA((CHUNKS,)),
            pltpu.SemaphoreType.DMA((CHUNKS,)),
            pltpu.SemaphoreType.DMA((2,)),
            pltpu.SemaphoreType.DMA((2,)),
            pltpu.SemaphoreType.DMA((2,)),
            pltpu.SemaphoreType.DMA((2,)),
        ],
        compiler_params=pltpu.CompilerParams(
            collective_id=0, has_side_effects=True, vmem_limit_bytes=50 << 20
        ),
    )(*operands)
    return pl.pallas_call(
        finish,
        out_shape=jax.ShapeDtypeStruct((2, ROWS, COLS), f32),
        in_specs=[vmem_spec] * 4,
        out_specs=hbm_spec,
        scratch_shapes=[
            pltpu.VMEM((2, ROWS, COLS), f32),
            pltpu.VMEM((2, 160, LANES), f32),
            pltpu.SemaphoreType.DMA((2 + len(LATE),)),
        ],
        compiler_params=pltpu.CompilerParams(vmem_limit_bytes=16 << 20),
    )(*first)


def solution(mesh):
    return jax.shard_map(
        on_device,
        mesh=mesh,
        in_specs=(P(None, "rg", "az"), P("rg"), P("rg", "az"), P("rg", "az")),
        out_specs=P(None, "rg", "az"),
        check_vma=False,
    )
```

```python
import math

import jax
import jax.numpy as jnp
import numpy as np
from jax import lax
from jax.experimental import pallas as pl
from jax.experimental.pallas import tpu as pltpu
from jax.sharding import PartitionSpec as P

MESH = pl.DeviceIdType.MESH
N_AZ = 64
N_RG = 4
ROWS = 512
COLS = 512
FULL = N_AZ * COLS
LANES = 128
FIRST = 256
SECOND = 128
CHUNKS = 4
CHUNK_ROWS = ROWS // CHUNKS
PAIR = CHUNK_ROWS // N_AZ
BLOCK = PAIR * 8
CHUNK_FLAT = N_AZ * BLOCK
FLAT = CHUNKS * CHUNK_FLAT
BEFORE = 8
AFTER = 72
FOCUS_ROWS = BEFORE + ROWS + AFTER + 8
TAPS = 15
EARLY = 7
LAST = 1
HALF_TILES = 8


def split(array):
    high = array.astype(jnp.bfloat16)
    low = (array - np.asarray(high).astype(np.float64)).astype(jnp.bfloat16)
    return high, low


def dft_tables():
    a = np.arange(FIRST)
    angle = 2.0 * np.pi * (np.outer(a, a) % FIRST) / FIRST
    cosine = np.cos(angle).reshape(FIRST, N_AZ, 4)
    sine = np.sin(angle).reshape(FIRST, N_AZ, 4)
    first = np.stack(
        [np.stack([cosine, sine], axis=2), np.stack([-sine, cosine], axis=2)], axis=0
    ).reshape(2 * FIRST, N_AZ * 8)
    angle = 2.0 * np.pi * (np.outer(a, np.arange(SECOND)) % FULL) / FULL
    norm = 1.0 / math.sqrt(FULL)
    twiddle = np.stack([np.cos(angle), np.sin(angle)]) * norm
    b = np.arange(SECOND)
    angle = 2.0 * np.pi * (np.outer(b, b) % SECOND) / SECOND
    cosine = np.cos(angle).reshape(N_AZ, 2, SECOND).transpose(1, 0, 2)
    sine = np.sin(angle).reshape(N_AZ, 2, SECOND).transpose(1, 0, 2)
    second = np.stack(
        [np.concatenate([cosine, sine], axis=2), np.concatenate([-sine, cosine], axis=2)], axis=0
    ).reshape(2 * SECOND, 2 * SECOND)
    first_high, first_low = split(first)
    second_high, second_low = split(second)
    return first_high, first_low, second_high, second_low, twiddle.astype(np.float32)


def sin_cos_of(rest, count):
    sign = 1.0 - 2.0 * (count - 2.0 * jnp.floor(count * 0.5))
    square = rest * rest
    sine = -1.0 / math.factorial(11)
    for order in (9, 7, 5, 3, 1):
        sine = sine * square + (-1.0) ** (order // 2) / math.factorial(order)
    cosine = 1.0 / math.factorial(12)
    for order in (10, 8, 6, 4, 2, 0):
        cosine = cosine * square + (-1.0) ** (order // 2) / math.factorial(order)
    return sine * rest * sign, cosine * sign


def sin_cos(angle):
    count = jnp.floor(angle * (1.0 / math.pi) + 0.5)
    rest = (angle - count * 3.140625) - count * (math.pi - 3.140625)
    return sin_cos_of(rest, count)


def sin_cos_pi(turns):
    count = jnp.floor(turns + 0.5)
    return sin_cos_of((turns - count) * math.pi, count)


def dot3(table_high, table_low, value, contract_on):
    high = value.astype(jnp.bfloat16)
    low = (value - high.astype(jnp.float32)).astype(jnp.bfloat16)
    dims = (((1,), (contract_on,)), ((), ()))
    dot = lambda left, right: lax.dot_general(left, right, dims, preferred_element_type=jnp.float32)
    return dot(table_high, high) + (dot(table_high, low) + dot(table_low, high))


def map_rows(out_ref, focus, weights, coarse, window, seg, first, count):
    def body(tile, carry):
        index = seg * 4 + tile
        h = coarse[index]
        eight = h >= 8
        four = (h & 4) != 0
        two = (h & 2) != 0
        one = (h & 1) != 0
        taps = [jnp.broadcast_to(weights[index, m : m + 1, :], (8, LANES)) for m in range(TAPS)]
        for part in range(2):
            plane = part * 4 + tile
            need = count + 3
            base = (seg * 16 + first) * 8 if isinstance(seg, int) else pl.multiple_of((seg * 16 + first) * 8, 8)
            load = lambda i: focus[plane, pl.ds(base + i * 8, 8), :]
            tiles = [load(i) for i in range(need + 8)]
            step = [
                jnp.where(eight, tiles[i + 8], tiles[i]) if i < need else tiles[i]
                for i in range(need + 7)
            ]
            step = [jnp.where(four, step[i + 4], step[i]) for i in range(need + 3)]
            step = [jnp.where(two, step[i + 2], step[i]) for i in range(need + 1)]
            for i in range(need):
                window[part, i * 8 : i * 8 + 8, :] = jnp.where(one, step[i + 1], step[i])
            for i in range(count):
                total = None
                for m in range(TAPS):
                    term = taps[m] * window[part, i * 8 + 5 + m : i * 8 + 13 + m, :]
                    total = term if total is None else total + term
                out_ref[part, pl.ds(base + i * 8, 8), pl.ds(pl.multiple_of(tile * LANES, LANES), LANES)] = total
        return carry

    lax.fori_loop(0, 4, body, 0)


def kernel(
    echo_hbm, chirp_hbm, shift_hbm, tap_hbm, t1h_hbm, t1l_hbm, t2h_hbm, t2l_hbm, tw_hbm,
    out_ref, focus, weights, coarse,
    echo, chirp_ref, shift_ref, tap_ref, t1h, t1l, t2h, t2l, tw, out_flat, in_flat, spec_flat, back_flat, phase_cos, phase_sin,
    chirp_cos, chirp_sin, window,
    load_sem, table_sem, send1, recv1, send2, recv2, halo_send, halo_recv, half_send, half_recv,
):
    me = lax.axis_index("az")
    rg = lax.axis_index("rg")
    up = lax.rem(rg + 1, N_RG)
    down = lax.rem(rg + N_RG - 1, N_RG)

    barrier = pltpu.get_barrier_semaphore()

    def moved(dz, rest):
        x, z, core = me // 16, me // 2 % 8, me % 2
        return ((x + rest // 2) % 4 * 8 + (z + dz) % 8) * 2 + (core + rest) % 2

    def around(i):
        return lax.rem(me + i, N_AZ)

    def nearest_first(i):
        rank = 7 - i // 8
        return moved(4 + (1 - rank % 2 * 2) * ((rank + 1) // 2), i % 8)

    def greet(i, carry):
        pl.semaphore_signal(
            barrier, inc=1, device_id=(lax.rem(me + i, N_AZ), rg), device_id_type=MESH
        )
        return carry

    chirp_copy = pltpu.make_async_copy(chirp_hbm, chirp_ref, table_sem.at[5])
    chirp_copy.start()
    echo_copies = []
    for chunk in range(CHUNKS):
        rows = pl.ds(chunk * CHUNK_ROWS, CHUNK_ROWS)
        echo_copies.append(
            pltpu.make_async_copy(echo_hbm.at[:, rows], echo.at[:, rows], load_sem.at[chunk])
        )
        echo_copies[-1].start()
    lax.fori_loop(1, N_AZ, greet, 0)
    for other in (up, down):
        pl.semaphore_signal(barrier, inc=1, device_id=(me, other), device_id_type=MESH)
    table_copies = []
    for index, (source, target) in enumerate(
        (
            (t1h_hbm, t1h), (t1l_hbm, t1l), (t2h_hbm, t2h), (t2l_hbm, t2l), (tw_hbm, tw),
        )
    ):
        table_copies.append(pltpu.make_async_copy(source, target, table_sem.at[index]))
        table_copies[-1].start()

    shift_copy = pltpu.make_async_copy(shift_hbm, shift_ref, table_sem.at[6])
    tap_copy = pltpu.make_async_copy(tap_hbm, tap_ref, table_sem.at[7])
    shift_copy.start()
    tap_copy.start()

    chirp_copy.wait()
    sine, cosine = sin_cos_pi(chirp_ref[...] * (1.0 / math.pi))
    for part in range(ROWS // LANES):
        rows = pl.ds(part * LANES, LANES)
        chirp_cos[rows, :] = jnp.transpose(
            jnp.broadcast_to(cosine[part : part + 1, :], (LANES, LANES))
        )
        chirp_sin[rows, :] = jnp.transpose(
            jnp.broadcast_to(sine[part : part + 1, :], (LANES, LANES))
        )

    def matched(chunk):
        def body(i, carry):
            row = pl.multiple_of(chunk * CHUNK_ROWS + i * 8, 8)
            c = chirp_cos[pl.ds(row, 8), :]
            s = chirp_sin[pl.ds(row, 8), :]
            for tile in range(4):
                lanes = slice(tile * LANES, (tile + 1) * LANES)
                re = echo[0, pl.ds(row, 8), lanes]
                im = echo[1, pl.ds(row, 8), lanes]
                out_flat[pl.ds(row * 8 + tile, 8, stride=8), :] = re * c + im * s
                out_flat[pl.ds(row * 8 + 4 + tile, 8, stride=8), :] = im * c - re * s
            return carry

        lax.fori_loop(0, CHUNK_ROWS // 8, body, 0)

    def exchange(source, target, send, recv, chunk, others=around):
        def body(i, carry):
            other = others(i)
            away = pl.multiple_of(chunk * CHUNK_FLAT + other * BLOCK, BLOCK)
            home = pl.multiple_of(chunk * CHUNK_FLAT + me * BLOCK, BLOCK)
            pltpu.make_async_remote_copy(
                src_ref=source.at[pl.ds(away, BLOCK)],
                dst_ref=target.at[pl.ds(home, BLOCK)],
                send_sem=send.at[chunk],
                recv_sem=recv.at[chunk],
                device_id=(other, rg),
                device_id_type=MESH,
            ).start()
            return carry

        lax.fori_loop(1, N_AZ, body, 0)
        home = pl.multiple_of(chunk * CHUNK_FLAT + me * BLOCK, BLOCK)
        target[pl.ds(home, BLOCK), :] = source[pl.ds(home, BLOCK), :]

    def half_row(half, device):
        return pl.multiple_of(LAST * CHUNK_FLAT + half * CHUNK_FLAT // 2 + device * 8, 8)

    def own_row(half, device):
        return pl.multiple_of(LAST * CHUNK_FLAT + device * BLOCK + half * 8, 8)

    def exchange_half(
        source, source_row, target, target_row, send, recv, half, others=around, beside=None
    ):
        def body(i, carry):
            other = others(i)
            pltpu.make_async_remote_copy(
                src_ref=source.at[pl.ds(source_row(half, other), 8)],
                dst_ref=target.at[pl.ds(target_row(half, me), 8)],
                send_sem=send,
                recv_sem=recv,
                device_id=(other, rg),
                device_id_type=MESH,
            ).start()
            if beside is not None:
                beside(i - 1)
            return carry

        lax.fori_loop(1, N_AZ, body, 0)
        target[pl.ds(target_row(half, me), 8), :] = source[pl.ds(source_row(half, me), 8), :]

    def half_of(half):
        rows = pl.ds(LAST * CHUNK_FLAT + half * CHUNK_FLAT // 2, CHUNK_FLAT // 2 - 8)
        return pltpu.make_async_remote_copy(
            src_ref=spec_flat.at[rows],
            dst_ref=back_flat.at[rows],
            send_sem=half_send.at[half],
            recv_sem=half_recv.at[half],
            device_id=(lax.rem(me + 1, N_AZ), rg),
            device_id_type=MESH,
        )

    def all_of(source, target, send, recv, chunk):
        rows = pl.ds(pl.multiple_of(chunk * CHUNK_FLAT, BLOCK), CHUNK_FLAT - BLOCK)
        return pltpu.make_async_remote_copy(
            src_ref=source.at[rows],
            dst_ref=target.at[rows],
            send_sem=send.at[chunk],
            recv_sem=recv.at[chunk],
            device_id=(lax.rem(me + 1, N_AZ), rg),
            device_id_type=MESH,
        )

    echo_copies[0].wait()
    matched(0)
    pl.semaphore_wait(barrier, N_AZ + 1)
    exchange(out_flat, in_flat, send1, recv1, 0, nearest_first)
    echo_copies[3].wait()
    matched(3)
    exchange(out_flat, in_flat, send1, recv1, 3)
    for chunk in (2, 1):
        echo_copies[chunk].wait()
        matched(chunk)

    lane_id = lax.broadcasted_iota(jnp.int32, (8, LANES), 1)
    row_id = lax.broadcasted_iota(jnp.int32, (8, LANES), 0)

    def phase_body(i, carry):
        row = pl.multiple_of(i * 8, 8)
        r = 1.0 + (rg * ROWS + row + row_id).astype(jnp.float32) * (1.0 / (ROWS * N_RG))
        rr = r * r
        for tile in range(4):
            line = me * COLS + tile * LANES + lane_id
            signed = jnp.where(line < FULL // 2, line, line - FULL)
            q = signed.astype(jnp.float32) * (0.9 / (FULL // 2))
            s, c = sin_cos(40.0 * jnp.sqrt(rr - q * q))
            phase_cos[tile, pl.ds(row, 8), :] = c
            phase_sin[tile, pl.ds(row, 8), :] = s
        return carry

    lax.fori_loop(0, ROWS // 8, phase_body, 0)

    shift_copy.wait()
    tap_copy.wait()
    tap_id = lax.broadcasted_iota(jnp.int32, (16, LANES), 0)
    for seg in range(CHUNKS):
        for tile in range(4):
            lanes = slice(tile * LANES, (tile + 1) * LANES)
            shift = shift_ref[seg : seg + 1, lanes]
            slot = tap_id - jnp.broadcast_to(shift & 7, (16, LANES))
            frac = jnp.broadcast_to(tap_ref[seg : seg + 1, lanes], (16, LANES))
            u = (slot - 3).astype(jnp.float32) - frac.astype(jnp.float32) * (1.0 / 16.0)
            sine, _ = sin_cos_pi(u)
            _, cosine = sin_cos_pi(u * 0.25)
            at_zero = u == 0.0
            sinc = jnp.where(at_zero, 1.0, sine / jnp.where(at_zero, 1.0, u * math.pi))
            inside = jnp.logical_and(slot >= 0, slot < 8)
            weights[seg * 4 + tile] = jnp.where(inside, sinc * (0.54 + 0.46 * cosine), 0.0)
            coarse[seg * 4 + tile] = jnp.broadcast_to(shift >> 3, (8, LANES))

    for plane in range(8):
        focus[plane, pl.ds(BEFORE, ROWS), :] = jnp.zeros((ROWS, LANES), jnp.float32)
        focus[plane, pl.ds(BEFORE + ROWS + AFTER, 8), :] = jnp.zeros((8, LANES), jnp.float32)

    for copy in table_copies:
        copy.wait()

    def transform(chunk):
        all_of(out_flat, in_flat, send1, recv1, chunk).wait_recv()
        start = pl.multiple_of(chunk * CHUNK_FLAT, CHUNK_FLAT)
        both = in_flat[pl.ds(start, CHUNK_FLAT), :].reshape(N_AZ, PAIR, 8, LANES)
        signal = jnp.concatenate(
            [both[:, pair].reshape(N_AZ * 8, LANES) for pair in range(PAIR)], axis=1
        )
        section = dot3(t1h[...], t1l[...], signal, 0)
        for pair in range(PAIR):
            lanes = slice(pair * LANES, (pair + 1) * LANES)
            re = section[:FIRST, lanes]
            im = section[FIRST:, lanes]
            turned = jnp.concatenate([re * tw[0] + im * tw[1], im * tw[0] - re * tw[1]], axis=1)
            final = dot3(t2h[...], t2l[...], turned, 1)
            for quarter in range(4):
                for half in range(2):
                    spec_flat[pl.ds(start + pair * 8 + quarter * 2 + half, N_AZ, stride=BLOCK), :] = (
                        final[quarter * N_AZ : (quarter + 1) * N_AZ, half * LANES : (half + 1) * LANES]
                    )

        @pl.when(chunk != LAST)
        def _():
            exchange(spec_flat, back_flat, send2, recv2, chunk)

        @pl.when(chunk == LAST)
        def _():
            for half in (1, 0):
                exchange_half(
                    spec_flat, own_row, back_flat, half_row,
                    half_send.at[half], half_recv.at[half], half,
                )

    def focus_rows(chunk):
        all_of(spec_flat, back_flat, send2, recv2, chunk).wait_recv()
        focus_tiles(chunk * 16, 16)

    def focus_half(half):
        half_of(half).wait_recv()
        focus_tiles(LAST * 16 + half * HALF_TILES, HALF_TILES)

    def focus_tiles(first, count):
        def body(i, carry):
            row = pl.multiple_of((first + i) * 8, 8)
            for tile in range(4):
                a = back_flat[pl.ds(row * 8 + tile, 8, stride=8), :]
                b = back_flat[pl.ds(row * 8 + 4 + tile, 8, stride=8), :]
                c = phase_cos[tile, pl.ds(row, 8), :]
                s = phase_sin[tile, pl.ds(row, 8), :]
                focus[tile, pl.ds(BEFORE + row, 8), :] = a * c - b * s
                focus[4 + tile, pl.ds(BEFORE + row, 8), :] = a * s + b * c
            return carry

        lax.fori_loop(0, count, body, 0)

    def stolt(seg, first, count):
        map_rows(out_ref, focus, weights, coarse, window, seg, first, count)

    def halo(towards, source_row, target_row, which):
        def piece(plane, start, count):
            return pltpu.make_async_remote_copy(
                src_ref=focus.at[plane, pl.ds(source_row + start, count)],
                dst_ref=focus.at[plane, pl.ds(target_row + start, count)],
                send_sem=halo_send.at[which],
                recv_sem=halo_recv.at[which],
                device_id=(me, towards),
                device_id_type=MESH,
            )

        return piece

    down_piece = halo(down, BEFORE, BEFORE + ROWS, 0)
    up_piece = halo(up, BEFORE + ROWS - BEFORE, 0, 1)
    to_down = down_piece(slice(None), 0, AFTER)
    to_up = up_piece(slice(None), 0, BEFORE)

    def send_down(piece):
        down_piece(piece // 9, pl.multiple_of(piece % 9 * 8, 8), 8).start()

    def step(k, carry):
        now = (CHUNKS - k) % CHUNKS
        transform(now)

        @pl.when(k == 0)
        def _():
            exchange(out_flat, in_flat, send1, recv1, 2)

        @pl.when(k >= 1)
        def _():
            focus_rows((CHUNKS + 1 - k) % CHUNKS)

        @pl.when(k == 1)
        def _():
            first = out_flat, half_row, in_flat, own_row, send1.at[LAST], recv1.at[LAST]
            exchange_half(*first, 0, beside=send_down)
            exchange_half(*first, 1)
            for piece in range(N_AZ - 1, 72):
                send_down(piece)

        @pl.when(k == 2)
        def _():
            for plane in range(8):
                up_piece(plane, 0, BEFORE).start()
            to_down.wait_recv()

            @pl.when(rg == N_RG - 1)
            def _():
                focus[:, pl.ds(BEFORE + ROWS, AFTER), :] = jnp.zeros((8, AFTER, LANES), jnp.float32)

        @pl.when(k >= 2)
        def _():
            seg = CHUNKS + 1 - k
            stolt(seg, 1, EARLY - 1)
            stolt(seg, EARLY, 16 - EARLY)

        return carry

    lax.fori_loop(0, CHUNKS, step, 0)
    stolt(3, 0, 1)
    to_up.wait_recv()

    @pl.when(rg == 0)
    def _():
        focus[:, pl.ds(0, BEFORE), :] = jnp.zeros((8, BEFORE, LANES), jnp.float32)

    stolt(0, 0, EARLY)
    focus_half(1)
    stolt(LAST, HALF_TILES + 1, 7)
    stolt(2, 0, 1)
    focus_half(0)
    to_down.wait_send()
    to_up.wait_send()
    for chunk in range(CHUNKS):
        all_of(out_flat, in_flat, send1, recv1, chunk).wait_send()
        if chunk != LAST:
            all_of(spec_flat, back_flat, send2, recv2, chunk).wait_send()
    for half in range(2):
        half_of(half).wait_send()


LATE = ((0, EARLY, 16 - EARLY), (LAST, 0, HALF_TILES + 1))


def finish(part_ref, focus, weights, coarse, out_hbm, late, window, store_sem):
    copies = []

    def store(source, first, end):
        rows = pl.ds(first, end - first)
        copies.append(
            pltpu.make_async_copy(
                source.at[:, rows], out_hbm.at[:, rows], store_sem.at[len(copies)]
            )
        )
        copies[-1].start()

    store(part_ref, 0, EARLY * 8)
    store(part_ref, (LAST * 16 + HALF_TILES + 1) * 8, ROWS)
    for seg, first, count in LATE:
        map_rows(late, focus, weights, coarse, window, seg, first, count)
        store(late, (seg * 16 + first) * 8, (seg * 16 + first + count) * 8)
    for copy in copies:
        copy.wait()


def on_device(echo_data, chirp_phase, stolt_shift, tap_index):
    tables = [jnp.asarray(table) for table in dft_tables()]
    vmem_spec = pl.BlockSpec(memory_space=pltpu.VMEM)
    hbm_spec = pl.BlockSpec(memory_space=pltpu.HBM)
    f32 = jnp.float32
    chirp = chirp_phase.reshape(ROWS // LANES, LANES)
    operands = [
        pltpu.with_memory_space_constraint(operand, pltpu.HBM)
        for operand in (echo_data, chirp, stolt_shift, tap_index, *tables)
    ]
    first = pl.pallas_call(
        kernel,
        out_shape=[
            pltpu.VMEM((2, ROWS, COLS), f32),
            pltpu.VMEM((8, FOCUS_ROWS, LANES), f32),
            pltpu.VMEM((16, 16, LANES), f32),
            pltpu.VMEM((16, 8, LANES), jnp.int32),
        ],
        in_specs=[hbm_spec] * 9,
        out_specs=[vmem_spec] * 4,
        scratch_shapes=[
            pltpu.VMEM((2, ROWS, COLS), f32),
            pltpu.VMEM((ROWS // LANES, LANES), f32),
            pltpu.VMEM((CHUNKS, COLS), jnp.int32),
            pltpu.VMEM((CHUNKS, COLS), jnp.int32),
            pltpu.VMEM((512, 512), jnp.bfloat16),
            pltpu.VMEM((512, 512), jnp.bfloat16),
            pltpu.VMEM((256, 256), jnp.bfloat16),
            pltpu.VMEM((256, 256), jnp.bfloat16),
            pltpu.VMEM((2, FIRST, SECOND), f32),
            pltpu.VMEM((FLAT, LANES), f32),
            pltpu.VMEM((FLAT, LANES), f32),
            pltpu.VMEM((FLAT, LANES), f32),
            pltpu.VMEM((FLAT, LANES), f32),
            pltpu.VMEM((4, ROWS, LANES), f32),
            pltpu.VMEM((4, ROWS, LANES), f32),
            pltpu.VMEM((ROWS, LANES), f32),
            pltpu.VMEM((ROWS, LANES), f32),
            pltpu.VMEM((2, 160, LANES), f32),
            pltpu.SemaphoreType.DMA((CHUNKS,)),
            pltpu.SemaphoreType.DMA((8,)),
            pltpu.SemaphoreType.DMA((CHUNKS,)),
            pltpu.SemaphoreType.DMA((CHUNKS,)),
            pltpu.SemaphoreType.DMA((CHUNKS,)),
            pltpu.SemaphoreType.DMA((CHUNKS,)),
            pltpu.SemaphoreType.DMA((2,)),
            pltpu.SemaphoreType.DMA((2,)),
            pltpu.SemaphoreType.DMA((2,)),
            pltpu.SemaphoreType.DMA((2,)),
        ],
        compiler_params=pltpu.CompilerParams(
            collective_id=0, has_side_effects=True, vmem_limit_bytes=50 << 20
        ),
    )(*operands)
    return pl.pallas_call(
        finish,
        out_shape=jax.ShapeDtypeStruct((2, ROWS, COLS), f32),
        in_specs=[vmem_spec] * 4,
        out_specs=hbm_spec,
        scratch_shapes=[
            pltpu.VMEM((2, ROWS, COLS), f32),
            pltpu.VMEM((2, 160, LANES), f32),
            pltpu.SemaphoreType.DMA((2 + len(LATE),)),
        ],
        compiler_params=pltpu.CompilerParams(vmem_limit_bytes=16 << 20),
    )(*first)


def solution(mesh):
    return jax.shard_map(
        on_device,
        mesh=mesh,
        in_specs=(P(None, "rg", "az"), P("rg"), P("rg", "az"), P("rg", "az")),
        out_specs=P(None, "rg", "az"),
        check_vma=False,
    )
```
